128 devices in a mesh: dp: 4 (over y_hi, core), seq: 32 (over x, z, y_lo).
Axes of the slice: x: 4, y: 4 (y_hi: 2, y_lo: 2; y = y_hi * 2 + y_lo), z: 4, core: 2. Of those that a mesh axis runs over, the one named last changes fastest.
Arguments:
- images: bfloat16 [4, 3, 1024, 1024], P('dp', None, 'seq'), may hold values from -6 to 6
- boxes: int32 [4, 4], replicated, may hold values from 0 to 1024, as said below
- w_embed: bfloat16 [588, 1280], replicated, may hold values from -0.25 to 0.25
- pos_embed: bfloat16 [4096, 1280], P('seq'), may hold values from -3 to 3
- gain_attn: float32 [1280], replicated, may hold values from 0.1 to 1.9
- w_qkv: bfloat16 [1280, 3840], replicated, as said below
- w_attn_out: bfloat16 [1280, 1280], replicated, may hold values from -0.15625 to 0.15625
- gain_mlp: float32 [1280], replicated, may hold values from 0.1 to 1.9
- w_up: bfloat16 [1280, 5120], P(None, 'dp'), may hold values from -0.15625 to 0.15625
- w_down: bfloat16 [5120, 1280], P('dp'), may hold values from -0.078125 to 0.078125
Outputs:
- encoded: bfloat16 [4, 4096, 1280], P('dp', 'seq')
The draws below stay inside these ranges and needn't reach their ends.
Inputs may be any that keep to these rules, and one draw needn't show every extreme that they name: `boxes`: each row is (top, left, height, width) of a crop inside the 1024 x 1024 source image, with height and width at least 512; in every draw some image's box is the whole source image and another image's box is the lower right quarter (top and left 1024 // 2, height and width 1024 // 2). `w_qkv`: columns are the query, key and value projections in that order.
All inputs are finite; a program needn't handle non-finite values.
Results may differ from the reference program's by a relative error of at most 0.04.
Values may be sent and summed in bfloat16 or wider, within the bound.
A program may use at most 192 MiB of HBM per device.

```python
import math
import jax
import jax.numpy as jnp
from jax import lax

HEADS = 16
HEAD_DIM = 80
D = 1280
FF = 5120
PATCH = 14
CH = 3
SRC = 1024
P_SIZE = 64
OUT = 896
SEQ_LEN = 4096
PATCH_DIM = 588
IMAGES = 4


def draw_boxes(key, part):
    key = jax.random.fold_in(key, 5)
    first_key, second_key, third_key, fourth_key, fifth_key, sixth_key = jax.random.split(key, 6)
    height = jax.random.randint(first_key, (IMAGES,), SRC // 2, SRC + 1)
    breadth = jax.random.randint(second_key, (IMAGES,), SRC // 2, SRC + 1)
    top_edge = jax.random.randint(third_key, (IMAGES,), 0, SRC - height + 1)
    left_edge = jax.random.randint(fourth_key, (IMAGES,), 0, SRC - breadth + 1)
    chosen = jax.random.randint(fifth_key, (), 0, IMAGES)
    offset = jax.random.randint(sixth_key, (), 1, IMAGES)
    quarter_index = (chosen + offset) % IMAGES
    indices = jnp.arange(IMAGES, dtype=jnp.int32)
    whole = indices == chosen
    quarter = indices == quarter_index
    height = jnp.where(whole, SRC, jnp.where(quarter, SRC // 2, height))
    breadth = jnp.where(whole, SRC, jnp.where(quarter, SRC // 2, breadth))
    top_edge = jnp.where(whole, 0, jnp.where(quarter, SRC // 2, top_edge))
    left_edge = jnp.where(whole, 0, jnp.where(quarter, SRC // 2, left_edge))
    return jnp.stack([top_edge, left_edge, height, breadth], axis=1).astype(jnp.int32)


def draw_w_qkv(key, part):
    key = jax.random.fold_in(key, 11)
    query_key, other_key, value_key = jax.random.split(key, 3)
    scale = 2.0 / math.sqrt(D)
    queries = jax.random.truncated_normal(query_key, -4.0, 4.0, (D, D), jnp.float32) * scale
    values = jax.random.truncated_normal(value_key, -4.0, 4.0, (D, D), jnp.float32) / math.sqrt(D)
    keyset = jax.random.truncated_normal(other_key, -4.0, 4.0, (D, D), jnp.float32) * scale
    return jnp.concatenate([queries, keyset, values], axis=1).astype(jnp.bfloat16)


def level_of(rng, dims, cuts, smallest, top_value):
    level, own = 1.0, jax.random.fold_in(rng, 6)
    for position, blocks in cuts:
        heights = jnp.exp(jax.random.uniform(jax.random.fold_in(own, position), (blocks,), jnp.float32, smallest / len(cuts), top_value / len(cuts)))
        level = level * jnp.repeat(heights, dims[position] // blocks).reshape([-1 if axis == position else 1 for axis in range(len(dims))])
    return level


def normal_values(own_key, dims, scale, bound, pieces=(), kind=jnp.bfloat16):
    level = level_of(own_key, dims, pieces, -0.22, 0.18) if pieces else 1.0
    values = jax.random.normal(own_key, dims, jnp.float32) * scale * level
    return jnp.minimum(jnp.maximum(values, -bound), bound).astype(kind)


def setup_inputs(seed: int = 0) -> dict:
    streams_of = jax.random.split(jax.random.key(seed), 11)
    return {
        "images": normal_values(streams_of[0], (IMAGES, CH, SRC, SRC), 1.0, 6.0, ((0, 4), (2, 32))),
        "boxes": draw_boxes(jax.random.fold_in(streams_of[10], 71), 0),
        "w_embed": normal_values(streams_of[2], (PATCH_DIM, D), PATCH_DIM ** -0.5, 0.25),
        "pos_embed": normal_values(streams_of[3], (SEQ_LEN, D), 0.5, 3.0, ((0, 32),)),
        "gain_attn": jnp.clip(1.0 + 0.18 * jax.random.normal(streams_of[4], (D,), jnp.float32), 0.1, 1.9),
        "w_qkv": draw_w_qkv(jax.random.fold_in(streams_of[10], 71), 0),
        "w_attn_out": normal_values(streams_of[6], (D, D), D ** -0.5, 0.15625),
        "gain_mlp": jnp.clip(1.0 + 0.18 * jax.random.normal(streams_of[7], (D,), jnp.float32), 0.1, 1.9),
        "w_up": normal_values(streams_of[8], (D, FF), D ** -0.5, 0.15625, ((1, 4),)),
        "w_down": normal_values(streams_of[9], (FF, D), FF ** -0.5, 0.078125, ((0, 4),)),
    }


def bilinear(first, length, targets, sources, extent):
    numer = (2 * targets + 1) * length - extent
    lower = jnp.where(numer < 0, 0, numer // (2 * extent))
    remain = jnp.where(numer < 0, 0, numer - lower * 2 * extent)
    fraction = remain.astype(jnp.float32) / (2.0 * extent)
    upper = jnp.minimum(lower + 1, length - 1)
    near_hit = (sources[None, :] == (first + lower)[:, None]).astype(jnp.float32)
    far_hit = (sources[None, :] == (first + upper)[:, None]).astype(jnp.float32)
    return (1.0 - fraction)[:, None] * near_hit + fraction[:, None] * far_hit

def layer_norm(values, gain):
    center = values - lax.optimization_barrier(jnp.mean(values, axis=-1, keepdims=True))
    spread = lax.optimization_barrier(jnp.mean(center * center, axis=-1, keepdims=True))
    return (center * lax.rsqrt(spread + 1e-06) * gain).astype(jnp.bfloat16)

def reference(images, boxes, w_embed, pos_embed, gain_attn, w_qkv, w_attn_out, gain_mlp, w_up, w_down):
    targets = jnp.arange(OUT, dtype=jnp.int32)
    sources = jnp.arange(SRC, dtype=jnp.int32)
    inverse = 1.0 / math.sqrt(HEAD_DIM)

    def attend(triple):
        queries, keyset, valueset = triple
        scores = jnp.dot(queries, keyset.T, preferred_element_type=jnp.float32) * inverse
        peak = lax.optimization_barrier(jnp.max(scores, axis=1, keepdims=True))
        unnormed = jnp.exp(scores - peak)
        totals = lax.optimization_barrier(jnp.sum(unnormed, axis=1, keepdims=True))
        product = jnp.dot(unnormed.astype(jnp.bfloat16), valueset, preferred_element_type=jnp.float32)
        return (product / totals).astype(jnp.bfloat16)

    def one_image(pair):
        picture, crop_box = pair
        row_weights = bilinear(crop_box[0], crop_box[2], targets, sources, OUT)
        col_weights = bilinear(crop_box[1], crop_box[3], targets, sources, OUT)
        narrowed = jnp.einsum('crq,pq->crp', picture.astype(jnp.float32), col_weights, precision=lax.Precision.HIGH)
        resampled = jnp.einsum('or,crp->cop', row_weights, narrowed, precision=lax.Precision.HIGH)
        patches = resampled.astype(jnp.bfloat16).reshape(CH, P_SIZE, PATCH, P_SIZE, PATCH)
        patches = patches.transpose(1, 3, 0, 2, 4).reshape(SEQ_LEN, PATCH_DIM)
        embedded = jnp.dot(patches, w_embed, preferred_element_type=jnp.float32) + pos_embed.astype(jnp.float32)
        normed_attn = layer_norm(embedded, gain_attn)
        projected = jnp.dot(normed_attn, w_qkv, preferred_element_type=jnp.float32).astype(jnp.bfloat16)
        split_heads = projected.reshape(SEQ_LEN, 3, HEADS, HEAD_DIM).transpose(1, 2, 0, 3)
        attended = lax.map(attend, (split_heads[0], split_heads[1], split_heads[2]))
        attended = attended.transpose(1, 0, 2).reshape(SEQ_LEN, D)
        middle = embedded + jnp.dot(attended, w_attn_out, preferred_element_type=jnp.float32)
        normed_mlp = layer_norm(middle, gain_mlp)
        hidden = jax.nn.gelu(jnp.dot(normed_mlp, w_up, preferred_element_type=jnp.float32), approximate=False).astype(jnp.bfloat16)
        return (middle + jnp.dot(hidden, w_down, preferred_element_type=jnp.float32)).astype(jnp.bfloat16)
    return lax.map(one_image, (images, boxes))
```

```python
import functools
import math

import jax
import jax.numpy as jnp
from jax import lax
from jax.experimental import pallas as pl
from jax.experimental.pallas import tpu as pltpu
from jax.sharding import PartitionSpec as P

HEADS = 16
HEAD = 80
PATCH = 14
OUT = 896
SEQ = 32
TOK = 128
WIDTH = 1280
MESH = pl.DeviceIdType.MESH
F32 = jnp.float32
BF16 = jnp.bfloat16


def taps(o, valid, first, length):
    numer = ((2 * o + 1) * length - OUT).astype(F32)
    lower = jnp.floor(numer * (1.0 / (2 * OUT)))
    remain = numer - lower * (2.0 * OUT)
    lower = jnp.where(remain < 0, lower - 1.0, jnp.where(remain >= 2.0 * OUT, lower + 1.0, lower))
    remain = numer - lower * (2.0 * OUT)
    lower = jnp.where(numer < 0, 0.0, lower).astype(jnp.int32)
    share = jnp.where(numer < 0, 0.0, remain) * (1.0 / (2 * OUT))
    upper = jnp.minimum(lower + 1, length - 1)
    near = jnp.where(valid, first + lower, -1)
    far = jnp.where(valid, first + upper, -1)
    return near, far, share


def resample_kernel(boxes, img, out, wcol, cmat, send1, recv1, wrow, send2, recv2, wide, s1, r1, s2, r2):
    dp, me = lax.axis_index("dp"), lax.axis_index("seq")
    barrier = pltpu.get_barrier_semaphore()

    @pl.loop(1, SEQ)
    def _(k):
        pl.semaphore_signal(barrier, inc=1, device_id=(dp, lax.rem(me + k, SEQ)), device_id_type=MESH)

    top, left, height, width = boxes[dp, 0], boxes[dp, 1], boxes[dp, 2], boxes[dp, 3]

    @pl.loop(0, 8)
    def _(t):
        lane = lax.broadcasted_iota(jnp.int32, (8, 128), 1)
        half, d4, j = lane // 64, (lane % 64) // 16, lane % 16
        o = (t * 4 + d4) * 28 + half * 14 + j
        near, far, share = taps(o, j < 14, left, width)
        near, far, share = near[:1], far[:1], share[:1]
        row = lax.broadcasted_iota(jnp.int32, (1024, 128), 0)
        w = jnp.where(row == near, 1.0 - share, 0.0) + jnp.where(row == far, share, 0.0)
        wcol[:, pl.ds(pl.multiple_of(t * 128, 128), 128)] = w.astype(BF16)

    cmat[...] = jnp.dot(img[...], wcol[...], preferred_element_type=F32)

    @pl.loop(0, 8)
    def _(t):
        cols = pl.ds(pl.multiple_of(t * 128, 128), 128)
        lane = lax.broadcasted_iota(jnp.int32, (32, 128), 1)
        group = (lane % 64) // 16
        parts = [cmat[32 * ch : 32 * ch + 32, cols] for ch in range(3)]
        for d4 in range(4):
            chunk = jnp.zeros((32, 128), F32)
            for ch in range(3):
                shift = (16 * (ch - d4)) % 128
                moved = parts[ch] if shift == 0 else pltpu.roll(parts[ch], shift, 1)
                chunk = jnp.where(group == ch, moved, chunk)
            send1[t * 4 + d4] = chunk.astype(BF16)

    def first(dst, src):
        return pltpu.make_async_remote_copy(
            src_ref=send1.at[dst], dst_ref=recv1.at[src], send_sem=s1.at[dst], recv_sem=r1.at[src],
            device_id=(dp, dst), device_id_type=MESH)

    def second(dst, src):
        return pltpu.make_async_remote_copy(
            src_ref=send2.at[dst], dst_ref=recv2.at[src], send_sem=s2.at[dst], recv_sem=r2.at[src],
            device_id=(dp, dst), device_id_type=MESH)

    pl.semaphore_wait(barrier, SEQ - 1)

    @pl.loop(1, SEQ)
    def _(k):
        first(lax.rem(me + k, SEQ), me).start()

    recv1[me] = send1[me]

    @pl.loop(0, 8)
    def _(t):
        row = lax.broadcasted_iota(jnp.int32, (128, 128), 0) + t * 128
        odd, d, kt, a2 = row // 512, (row % 512) // 16, (row % 16) // 2, row % 2
        o = (2 * d + a2) * 14 + 2 * kt + odd
        near, far, share = taps(o, kt < 7, top, height)
        rows = pl.ds(pl.multiple_of(t * 128, 128), 128)
        for c in range(8):
            col = lax.broadcasted_iota(jnp.int32, (128, 128), 1) + c * 128
            w = jnp.where(col == near, 1.0 - share, 0.0) + jnp.where(col == far, share, 0.0)
            wrow[rows, c * 128 : c * 128 + 128] = w.astype(BF16)

    @pl.loop(1, SEQ)
    def _(k):
        first(me, lax.rem(me + k, SEQ)).wait_recv()

    x = recv1[...].reshape(1024, 128)
    even = jnp.dot(wrow[:512], x, preferred_element_type=F32)
    odd = jnp.dot(wrow[512:], x, preferred_element_type=F32)
    low = lax.broadcasted_iota(jnp.int32, (512, 128), 1) < 64
    send2[:, 0] = jnp.where(low, even, pltpu.roll(odd, 64, 1)).astype(BF16).reshape(32, 16, 128)
    send2[:, 1] = jnp.where(low, pltpu.roll(even, 64, 1), odd).astype(BF16).reshape(32, 16, 128)

    @pl.loop(1, SEQ)
    def _(k):
        second(lax.rem(me + k, SEQ), me).start()

    recv2[me] = send2[me]

    @pl.loop(1, SEQ)
    def _(k):
        first(lax.rem(me + k, SEQ), me).wait_send()
        second(me, lax.rem(me + k, SEQ)).wait_recv()

    wide[...] = recv2[...].reshape(1024, 128).astype(F32)
    for kt in range(7):
        for a2 in range(2):
            piece = wide[pl.ds(kt * 2 + a2, 64, stride=16), :]
            out[a2 * 64 : a2 * 64 + 64, kt * 128 : kt * 128 + 128] = piece.astype(BF16)

    @pl.loop(1, SEQ)
    def _(k):
        second(lax.rem(me + k, SEQ), me).wait_send()


def resample(boxes, img):
    return pl.pallas_call(
        resample_kernel,
        out_shape=jax.ShapeDtypeStruct((TOK, OUT), BF16),
        in_specs=[pl.BlockSpec(memory_space=pltpu.SMEM), pl.BlockSpec(memory_space=pltpu.VMEM)],
        out_specs=pl.BlockSpec(memory_space=pltpu.VMEM),
        scratch_shapes=[
            pltpu.VMEM((1024, 1024), BF16),
            pltpu.VMEM((96, 1024), F32),
            pltpu.VMEM((SEQ, 32, 128), BF16),
            pltpu.VMEM((SEQ, 32, 128), BF16),
            pltpu.VMEM((1024, 1024), BF16),
            pltpu.VMEM((SEQ, 2, 16, 128), BF16),
            pltpu.VMEM((SEQ, 2, 16, 128), BF16),
            pltpu.VMEM((1024, 128), F32),
            pltpu.SemaphoreType.DMA((SEQ,)),
            pltpu.SemaphoreType.DMA((SEQ,)),
            pltpu.SemaphoreType.DMA((SEQ,)),
            pltpu.SemaphoreType.DMA((SEQ,)),
        ],
        compiler_params=pltpu.CompilerParams(
            collective_id=0, has_side_effects=True, vmem_limit_bytes=48 * 1024 * 1024),
        name="resample",
    )(boxes, img)


QB = 256


def attend_kernel(proj, out, flat, mine, theirs, acc, peak, back, s_in, r_in, s_swap, r_swap, s_back, r_back):
    dp, me = lax.axis_index("dp"), lax.axis_index("seq")
    core, base = lax.rem(dp, 2), dp - lax.rem(dp, 2)
    half, slot = lax.rem(me, 2), me // 2
    image, head = me // 16, lax.rem(me, 16)
    to_dp, to_seq = base + half, core * 16
    from_dp = base + image
    sibling = base + 1 - core

    barrier = pltpu.get_barrier_semaphore()

    def is_me(d, s):
        return jnp.logical_and(d == dp, s == me)

    for h in range(HEADS):
        @pl.when(jnp.logical_not(is_me(to_dp, to_seq + h)))
        def _():
            pl.semaphore_signal(barrier, inc=1, device_id=(to_dp, to_seq + h), device_id_type=MESH)

        @pl.when(jnp.logical_not(is_me(from_dp, 2 * h + core)))
        def _():
            pl.semaphore_signal(barrier, inc=1, device_id=(from_dp, 2 * h + core), device_id_type=MESH)
    pl.semaphore_signal(barrier, inc=1, device_id=(sibling, me), device_id_type=MESH)

    mine[2, HEAD:, :] = jnp.ones((16, 2048), BF16)
    mine[1, HEAD:, :] = jnp.zeros((16, 2048), BF16)
    mine[0, HEAD:, :] = jnp.zeros((16, 2048), BF16)

    for t in range(3):
        for j in range(10):
            block = proj[:, t * WIDTH + j * 128 : t * WIDTH + j * 128 + 128].astype(F32)
            if t == 0:
                block = block * (math.log2(math.e) / math.sqrt(HEAD))
            flat[t, j * 128 : j * 128 + 128, :] = block.T.astype(BF16)

    self_head = jnp.logical_and(to_dp == dp, core == image)
    both = jnp.where(self_head, 2 * 15 + 1, 2 * 16 + 1)
    pl.semaphore_wait(barrier, both)

    def rows(h):
        return pl.ds(pl.multiple_of(h * HEAD, 16), HEAD)

    def lanes(i):
        return pl.ds(pl.multiple_of(i * TOK, TOK), TOK)

    def inward(h, i):
        return pltpu.make_async_remote_copy(
            src_ref=flat.at[:, rows(h), :], dst_ref=mine.at[:, pl.ds(0, HEAD), lanes(i)],
            send_sem=s_in.at[h], recv_sem=r_in.at[i],
            device_id=(to_dp, to_seq + h), device_id_type=MESH)

    def backward(i, h):
        return pltpu.make_async_remote_copy(
            src_ref=back.at[i], dst_ref=out.at[rows(h), :],
            send_sem=s_back.at[i], recv_sem=r_back.at[h],
            device_id=(from_dp, 2 * i + core), device_id_type=MESH)

    swap = pltpu.make_async_remote_copy(
        src_ref=mine.at[pl.ds(1, 2)], dst_ref=theirs, send_sem=s_swap, recv_sem=r_swap,
        device_id=(sibling, me), device_id_type=MESH)

    @pl.loop(0, HEADS)
    def _(k):
        h = lax.rem(slot + k, HEADS)

        @pl.when(is_me(to_dp, to_seq + h))
        def _():
            pltpu.make_async_copy(
                flat.at[:, rows(h), :], mine.at[:, pl.ds(0, HEAD), lanes(slot)], r_in.at[slot]).start()

        @pl.when(jnp.logical_not(is_me(to_dp, to_seq + h)))
        def _():
            inward(h, slot).start()

    @pl.loop(0, HEADS)
    def _(i):
        inward(0, i).wait_recv()

    swap.start()

    def scan(queries, keys, values):
        s = jnp.dot(queries, keys, preferred_element_type=F32)
        m = jnp.max(s, axis=1, keepdims=True)
        p = jnp.exp2(s - m).astype(BF16)
        o = lax.dot_general(p, values, (((1,), (1,)), ((), ())), preferred_element_type=F32)
        return m, o

    @pl.loop(0, 2048 // QB)
    def _(b):
        q = mine[0, :, pl.ds(pl.multiple_of(b * QB, QB), QB)].astype(F32).T.astype(BF16)
        m, o = scan(q, mine[1], mine[2])
        here = pl.ds(pl.multiple_of(b * QB, QB), QB)
        peak[here, :] = jnp.broadcast_to(m, (QB, 128))
        acc[here, :] = o

    swap.wait_recv()

    @pl.loop(0, 2048 // QB)
    def _(b):
        q = mine[0, :, pl.ds(pl.multiple_of(b * QB, QB), QB)].astype(F32).T.astype(BF16)
        m2, o2 = scan(q, theirs[0], theirs[1])
        here = pl.ds(pl.multiple_of(b * QB, QB), QB)
        m1 = peak[here, :][:, :1]
        o1 = acc[here, :]
        m = jnp.maximum(m1, m2)
        o = o1 * jnp.exp2(m1 - m) + o2 * jnp.exp2(m2 - m)
        o = o / o[:, HEAD : HEAD + 1]
        for j in range(QB // TOK):
            i = b * (QB // TOK) + j
            back[i] = o[j * TOK : j * TOK + TOK, :].T[:HEAD].astype(BF16)

            @pl.when(is_me(from_dp, 2 * i + core))
            def _():
                pltpu.make_async_copy(back.at[i], out.at[rows(head), :], r_back.at[head]).start()

            @pl.when(jnp.logical_not(is_me(from_dp, 2 * i + core)))
            def _():
                backward(i, head).start()

    swap.wait_send()

    @pl.loop(0, HEADS)
    def _(h):
        backward(0, h).wait_recv()

        @pl.when(jnp.logical_not(is_me(to_dp, to_seq + h)))
        def _():
            inward(h, 0).wait_send()

        @pl.when(jnp.logical_not(is_me(from_dp, 2 * h + core)))
        def _():
            backward(h, 0).wait_send()


def attend(proj):
    return pl.pallas_call(
        attend_kernel,
        out_shape=jax.ShapeDtypeStruct((WIDTH, TOK), BF16),
        in_specs=[pl.BlockSpec(memory_space=pltpu.VMEM)],
        out_specs=pl.BlockSpec(memory_space=pltpu.VMEM),
        scratch_shapes=[
            pltpu.VMEM((3, WIDTH, TOK), BF16),
            pltpu.VMEM((3, 96, 2048), BF16),
            pltpu.VMEM((2, 96, 2048), BF16),
            pltpu.VMEM((2048, 96), F32),
            pltpu.VMEM((2048, 128), F32),
            pltpu.VMEM((16, HEAD, TOK), BF16),
            pltpu.SemaphoreType.DMA((16,)),
            pltpu.SemaphoreType.DMA((16,)),
            pltpu.SemaphoreType.DMA,
            pltpu.SemaphoreType.DMA,
            pltpu.SemaphoreType.DMA((16,)),
            pltpu.SemaphoreType.DMA((16,)),
        ],
        compiler_params=pltpu.CompilerParams(
            collective_id=1, has_side_effects=True, vmem_limit_bytes=56 * 1024 * 1024),
        name="attend",
    )(proj)


def layer_norm(values, gain):
    center = values - jnp.mean(values, axis=-1, keepdims=True)
    spread = jnp.mean(center * center, axis=-1, keepdims=True)
    return (center * lax.rsqrt(spread + 1e-06) * gain).astype(BF16)


def shards(images, boxes, w_embed, pos_embed, gain_attn, w_qkv, w_attn_out, gain_mlp, w_up, w_down):
    tokens = resample(boxes, images.reshape(96, 1024))
    w = w_embed.reshape(3, PATCH, PATCH, WIDTH).transpose(1, 0, 2, 3)
    w = jnp.pad(w, ((0, 0), (0, 1), (0, 2), (0, 0))).reshape(OUT, WIDTH)
    embedded = jnp.dot(tokens, w, preferred_element_type=F32) + pos_embed.astype(F32)
    normed_attn = layer_norm(embedded, gain_attn)
    projected = jnp.dot(normed_attn, w_qkv, preferred_element_type=F32).astype(BF16)
    attended = attend(projected)
    middle = embedded + lax.dot_general(
        attended, w_attn_out, (((0,), (0,)), ((), ())), preferred_element_type=F32)
    normed_mlp = layer_norm(middle, gain_mlp)
    gathered = lax.all_gather(normed_mlp, "dp", axis=0, tiled=True)
    hidden = jax.nn.gelu(
        jnp.dot(gathered, w_up, preferred_element_type=F32), approximate=False).astype(BF16)
    mixed = lax.psum_scatter(
        jnp.dot(hidden, w_down, preferred_element_type=F32).astype(BF16),
        "dp", scatter_dimension=0, tiled=True).astype(F32)
    return (middle + mixed).astype(BF16)[None]


def solution(mesh):
    return jax.shard_map(
        shards,
        mesh=mesh,
        in_specs=(
            P("dp", None, "seq", None), P(), P(), P("seq", None), P(), P(), P(), P(),
            P(None, "dp"), P("dp", None),
        ),
        out_specs=P("dp", "seq", None),
        check_vma=False,
    )
```

```python
import math

import jax
import jax.numpy as jnp
from jax import lax
from jax.experimental import pallas as pl
from jax.experimental.pallas import tpu as pltpu
from jax.sharding import PartitionSpec as P

HEADS = 16
HEAD = 80
PATCH = 14
OUT = 896
SEQ = 32
TOK = 128
WIDTH = 1280
MESH = pl.DeviceIdType.MESH
F32 = jnp.float32
BF16 = jnp.bfloat16


def taps(o, valid, first, length):
    numer = ((2 * o + 1) * length - OUT).astype(F32)
    lower = jnp.floor(numer * (1.0 / (2 * OUT)))
    remain = numer - lower * (2.0 * OUT)
    lower = jnp.where(remain < 0, lower - 1.0, jnp.where(remain >= 2.0 * OUT, lower + 1.0, lower))
    remain = numer - lower * (2.0 * OUT)
    lower = jnp.where(numer < 0, 0.0, lower).astype(jnp.int32)
    share = jnp.where(numer < 0, 0.0, remain) * (1.0 / (2 * OUT))
    upper = jnp.minimum(lower + 1, length - 1)
    near = jnp.where(valid, first + lower, -1)
    far = jnp.where(valid, first + upper, -1)
    return near, far, share


def layer_norm(values, gain):
    center = values - jnp.mean(values, axis=-1, keepdims=True)
    spread = jnp.mean(center * center, axis=-1, keepdims=True)
    return (center * lax.rsqrt(spread + 1e-06) * gain).astype(BF16)


def gelu(x):
    return 0.5 * x * (1.0 + lax.erf(x * (1.0 / math.sqrt(2.0))))


QB = 256
CHUNKS = 2
ROWS = TOK // CHUNKS


def layer_kernel(
    boxes, images, w_embed, pos_embed, gain_attn, w_qkv, w_out, gain_mlp, w_up, w_down, result,
    img, emb, pos, qkv, outw, upw, downw, load,
    wcol, cmat, send1, recv1, wrow, send2, recv2, wide, tokens, embw, embedded, s1, r1, s2, r2,
    flat, mine, theirs, acc, peak, back, heads, s_in, r_in, s_swap, r_swap, s_back, r_back,
    normed, near_tok, far_tok, far_near, total, give, fromnear, giveswap, fromswap, giveback, fromfar,
    s_near, r_near, s_far, r_far, s_relay, r_relay, s_give, r_give, s_gs, r_gs, s_gb, r_gb,
):
    dp, me = lax.axis_index("dp"), lax.axis_index("seq")
    core, base = lax.rem(dp, 2), dp - lax.rem(dp, 2)
    half, slot = lax.rem(me, 2), me // 2
    image, head = me // 16, lax.rem(me, 16)
    to_dp, to_seq = base + half, core * 16
    from_dp = base + image
    sibling = (base + 1 - core, me)
    partner = (2 - base + core, me + 1 - 2 * half)

    def is_me(d, s):
        return jnp.logical_and(d == dp, s == me)

    loads = [
        pltpu.make_async_copy(a, b, load.at[i])
        for i, (a, b) in enumerate((
            (images.at[0, 0], img.at[pl.ds(0, 32)]), (images.at[0, 1], img.at[pl.ds(32, 32)]),
            (images.at[0, 2], img.at[pl.ds(64, 32)]), (w_embed, emb), (pos_embed, pos), (w_qkv, qkv),
            (w_out, outw), (w_up, upw), (w_down, downw)))
    ]
    for one in loads:
        one.start()

    barrier = pltpu.get_barrier_semaphore()

    def greet(d, s):
        pl.semaphore_signal(barrier, inc=1, device_id=(d, s), device_id_type=MESH)

    @pl.loop(1, SEQ)
    def _(k):
        greet(dp, lax.rem(me + k, SEQ))

    @pl.loop(0, HEADS)
    def _(h):
        @pl.when(jnp.logical_not(is_me(to_dp, to_seq + h)))
        def _():
            greet(to_dp, to_seq + h)

        @pl.when(jnp.logical_not(is_me(from_dp, 2 * h + core)))
        def _():
            greet(from_dp, 2 * h + core)

    greet(*sibling)
    greet(*partner)

    top, left, height, width = boxes[dp, 0], boxes[dp, 1], boxes[dp, 2], boxes[dp, 3]

    @pl.loop(0, 8)
    def _(t):
        lane = lax.broadcasted_iota(jnp.int32, (8, 128), 1)
        part, d4, j = lane // 64, (lane % 64) // 16, lane % 16
        o = (t * 4 + d4) * 28 + part * 14 + j
        near, far, share = taps(o, j < 14, left, width)
        near, far, share = near[:1], far[:1], share[:1]
        row = lax.broadcasted_iota(jnp.int32, (1024, 128), 0)
        w = jnp.where(row == near, 1.0 - share, 0.0) + jnp.where(row == far, share, 0.0)
        wcol[:, pl.ds(pl.multiple_of(t * 128, 128), 128)] = w.astype(BF16)

    for one in loads[:3]:
        one.wait()
    cmat[...] = jnp.dot(img[...], wcol[...], preferred_element_type=F32)

    @pl.loop(0, 8)
    def _(t):
        cols = pl.ds(pl.multiple_of(t * 128, 128), 128)
        lane = lax.broadcasted_iota(jnp.int32, (32, 128), 1)
        group = (lane % 64) // 16
        parts = [cmat[32 * ch : 32 * ch + 32, cols] for ch in range(3)]
        for d4 in range(4):
            chunk = jnp.zeros((32, 128), F32)
            for ch in range(3):
                shift = (16 * (ch - d4)) % 128
                moved = parts[ch] if shift == 0 else pltpu.roll(parts[ch], shift, 1)
                chunk = jnp.where(group == ch, moved, chunk)
            send1[t * 4 + d4] = chunk.astype(BF16)

    def first(dst, src):
        return pltpu.make_async_remote_copy(
            src_ref=send1.at[dst], dst_ref=recv1.at[src], send_sem=s1.at[dst], recv_sem=r1.at[src],
            device_id=(dp, dst), device_id_type=MESH)

    def second(dst, src):
        return pltpu.make_async_remote_copy(
            src_ref=send2.at[dst], dst_ref=recv2.at[src], send_sem=s2.at[dst], recv_sem=r2.at[src],
            device_id=(dp, dst), device_id_type=MESH)

    self_head = jnp.logical_and(half == core, core == image)
    pl.semaphore_wait(barrier, SEQ - 1 + 2 + jnp.where(self_head, 2 * 15, 2 * 16))

    @pl.loop(1, SEQ)
    def _(k):
        first(lax.rem(me + k, SEQ), me).start()

    recv1[me] = send1[me]

    @pl.loop(0, 8)
    def _(t):
        row = lax.broadcasted_iota(jnp.int32, (128, 128), 0) + t * 128
        odd, d, kt, a2 = row // 512, (row % 512) // 16, (row % 16) // 2, row % 2
        o = (2 * d + a2) * 14 + 2 * kt + odd
        near, far, share = taps(o, kt < 7, top, height)
        rows = pl.ds(pl.multiple_of(t * 128, 128), 128)
        for c in range(8):
            col = lax.broadcasted_iota(jnp.int32, (128, 128), 1) + c * 128
            w = jnp.where(col == near, 1.0 - share, 0.0) + jnp.where(col == far, share, 0.0)
            wrow[rows, c * 128 : c * 128 + 128] = w.astype(BF16)

    @pl.loop(1, SEQ)
    def _(k):
        first(me, lax.rem(me + k, SEQ)).wait_recv()

    x = recv1[...].reshape(1024, 128)
    even = jnp.dot(wrow[:512], x, preferred_element_type=F32)
    odd = jnp.dot(wrow[512:], x, preferred_element_type=F32)
    low = lax.broadcasted_iota(jnp.int32, (512, 128), 1) < 64
    send2[:, 0] = jnp.where(low, even, pltpu.roll(odd, 64, 1)).astype(BF16).reshape(32, 16, 128)
    send2[:, 1] = jnp.where(low, pltpu.roll(even, 64, 1), odd).astype(BF16).reshape(32, 16, 128)

    @pl.loop(1, SEQ)
    def _(k):
        second(lax.rem(me + k, SEQ), me).start()

    recv2[me] = send2[me]

    for one in loads[3:5]:
        one.wait()

    @pl.loop(0, 7)
    def _(t):
        rho = lax.broadcasted_iota(jnp.int32, (128, 588), 0) + t * 128
        i, ch, j = rho // 64, (rho % 64) // 16, rho % 16
        origin = jnp.where(jnp.logical_and(ch < 3, j < 14), ch * 196 + i * 14 + j, -1)
        kappa = lax.broadcasted_iota(jnp.int32, (128, 588), 1)
        pick = jnp.where(origin == kappa, 1.0, 0.0).astype(BF16)
        rows = pl.ds(pl.multiple_of(t * 128, 128), 128)
        embw[rows, :] = jnp.dot(pick, emb[...], preferred_element_type=F32).astype(BF16)

    mine[0, HEAD:, :] = jnp.zeros((16, 2048), BF16)
    mine[1, HEAD:, :] = jnp.zeros((16, 2048), BF16)
    mine[2, HEAD:, :] = jnp.ones((16, 2048), BF16)

    @pl.loop(1, SEQ)
    def _(k):
        first(lax.rem(me + k, SEQ), me).wait_send()
        second(me, lax.rem(me + k, SEQ)).wait_recv()

    wide[...] = recv2[...].reshape(1024, 128).astype(F32)
    for kt in range(7):
        for a2 in range(2):
            piece = wide[pl.ds(kt * 2 + a2, 64, stride=16), :]
            tokens[a2 * 64 : a2 * 64 + 64, kt * 128 : kt * 128 + 128] = piece.astype(BF16)

    embedded[...] = jnp.dot(tokens[...], embw[...], preferred_element_type=F32) + pos[...].astype(F32)
    normed[...] = layer_norm(embedded[...], gain_attn[...])

    def head_rows(h):
        return pl.ds(pl.multiple_of(h * HEAD, 16), HEAD)

    def lanes(i):
        return pl.ds(pl.multiple_of(i * TOK, TOK), TOK)

    def inward(t, h, i):
        return pltpu.make_async_remote_copy(
            src_ref=flat.at[t, head_rows(h), :], dst_ref=mine.at[t, pl.ds(0, HEAD), lanes(i)],
            send_sem=s_in.at[t, h], recv_sem=r_in.at[t, i],
            device_id=(to_dp, to_seq + h), device_id_type=MESH)

    def backward(i, h):
        return pltpu.make_async_remote_copy(
            src_ref=back.at[i], dst_ref=heads.at[head_rows(h), :],
            send_sem=s_back.at[i], recv_sem=r_back.at[h],
            device_id=(from_dp, 2 * i + core), device_id_type=MESH)

    loads[5].wait()
    for t in (1, 0, 2):
        proj = jnp.dot(normed[...], qkv[:, t * WIDTH : (t + 1) * WIDTH], preferred_element_type=F32)
        if t == 0:
            proj = proj * (math.log2(math.e) / math.sqrt(HEAD))
        for j in range(10):
            flat[t, j * 128 : j * 128 + 128, :] = proj[:, j * 128 : j * 128 + 128].T.astype(BF16)

        @pl.loop(0, HEADS)
        def _(k):
            h = lax.rem(slot + k, HEADS)

            @pl.when(is_me(to_dp, to_seq + h))
            def _():
                pltpu.make_async_copy(
                    flat.at[t, head_rows(h), :], mine.at[t, pl.ds(0, HEAD), lanes(slot)],
                    r_in.at[t, slot]).start()

            @pl.when(jnp.logical_not(is_me(to_dp, to_seq + h)))
            def _():
                inward(t, h, slot).start()

    @pl.loop(1, SEQ)
    def _(k):
        second(lax.rem(me + k, SEQ), me).wait_send()

    def swap(t):
        return pltpu.make_async_remote_copy(
            src_ref=mine.at[t + 1], dst_ref=theirs.at[t], send_sem=s_swap.at[t], recv_sem=r_swap.at[t],
            device_id=sibling, device_id_type=MESH)

    for t in (1, 0, 2):
        @pl.loop(0, HEADS)
        def _(i):
            inward(t, 0, i).wait_recv()

        if t > 0:
            swap(t - 1).start()

    def scan(queries, keys, values):
        s = jnp.dot(queries, keys, preferred_element_type=F32)
        m = jnp.max(s, axis=1, keepdims=True)
        p = jnp.exp2(s - m).astype(BF16)
        o = lax.dot_general(p, values, (((1,), (1,)), ((), ())), preferred_element_type=F32)
        return m, o

    @pl.loop(0, 2048 // QB)
    def _(b):
        q = mine[0, :, pl.ds(pl.multiple_of(b * QB, QB), QB)].astype(F32).T.astype(BF16)
        m, o = scan(q, mine[1], mine[2])
        here = pl.ds(pl.multiple_of(b * QB, QB), QB)
        peak[here, :] = jnp.broadcast_to(m, (QB, 128))
        acc[here, :] = o

    swap(0).wait_recv()
    swap(1).wait_recv()

    @pl.loop(0, 2048 // QB)
    def _(b):
        q = mine[0, :, pl.ds(pl.multiple_of(b * QB, QB), QB)].astype(F32).T.astype(BF16)
        m2, o2 = scan(q, theirs[0], theirs[1])
        here = pl.ds(pl.multiple_of(b * QB, QB), QB)
        m1 = peak[here, :][:, :1]
        o1 = acc[here, :]
        m = jnp.maximum(m1, m2)
        o = o1 * jnp.exp2(m1 - m) + o2 * jnp.exp2(m2 - m)
        o = o / o[:, HEAD : HEAD + 1]
        for j in range(QB // TOK):
            i = b * (QB // TOK) + j
            back[i] = o[j * TOK : j * TOK + TOK, :].T[:HEAD].astype(BF16)

            @pl.when(is_me(from_dp, 2 * i + core))
            def _():
                pltpu.make_async_copy(back.at[i], heads.at[head_rows(head), :], r_back.at[head]).start()

            @pl.when(jnp.logical_not(is_me(from_dp, 2 * i + core)))
            def _():
                backward(i, head).start()

    for one in loads[6:]:
        one.wait()

    @pl.loop(0, HEADS)
    def _(h):
        backward(0, h).wait_recv()

    attended = jnp.concatenate(
        [heads[j * 128 : j * 128 + 128, :].astype(F32).T.astype(BF16) for j in range(10)], axis=1)
    middle = embedded[...] + jnp.dot(attended, outw[...], preferred_element_type=F32)
    embedded[...] = middle
    normed[...] = layer_norm(middle, gain_mlp[...])

    def chunk(c):
        return pl.ds(c * ROWS, ROWS)

    def remote(src, dst, s, r, device):
        return pltpu.make_async_remote_copy(
            src_ref=src, dst_ref=dst, send_sem=s, recv_sem=r, device_id=device, device_id_type=MESH)

    def to_far(c):
        return remote(normed.at[chunk(c)], far_tok.at[chunk(c)], s_far.at[c], r_far.at[c], partner)

    def relay(c):
        return remote(far_tok.at[chunk(c)], far_near.at[chunk(c)], s_relay.at[c], r_relay.at[c], sibling)

    def swap_sum(c):
        return remote(giveswap.at[chunk(c)], fromswap.at[chunk(c)], s_gs.at[c], r_gs.at[c], sibling)

    def send_sum(c):
        return remote(giveback.at[chunk(c)], fromfar.at[chunk(c)], s_gb.at[c], r_gb.at[c], partner)

    to_near = remote(normed, near_tok, s_near, r_near, sibling)
    give_near = remote(give, fromnear, s_give, r_give, sibling)

    def mlp(x):
        hidden = gelu(jnp.dot(x, upw[...], preferred_element_type=F32)).astype(BF16)
        return jnp.dot(hidden, downw[...], preferred_element_type=F32)

    for c in range(CHUNKS):
        to_far(c).start()
    to_near.start()
    to_near.wait_recv()
    own = mlp(jnp.concatenate([normed[...], near_tok[...]], axis=0))
    total[...] = embedded[...] + own[:TOK]
    give[...] = own[TOK:].astype(BF16)
    give_near.start()

    to_far(0).wait_recv()
    relay(0).start()
    for c in range(CHUNKS):
        relay(c).wait_recv()
        sums = mlp(jnp.concatenate([far_tok[chunk(c), :], far_near[chunk(c), :]], axis=0))
        giveswap[chunk(c), :] = sums[ROWS:].astype(BF16)
        swap_sum(c).start()
        if c + 1 < CHUNKS:
            to_far(c + 1).wait_recv()
            relay(c + 1).start()
        swap_sum(c).wait_recv()
        giveback[chunk(c), :] = (sums[:ROWS] + fromswap[chunk(c), :].astype(F32)).astype(BF16)
        send_sum(c).start()

    give_near.wait_recv()
    total[...] = total[...] + fromnear[...].astype(F32)
    for c in range(CHUNKS):
        send_sum(c).wait_recv()
        result[chunk(c), :] = (total[chunk(c), :] + fromfar[chunk(c), :].astype(F32)).astype(BF16)

    to_near.wait_send()
    give_near.wait_send()
    swap(0).wait_send()
    swap(1).wait_send()
    for c in range(CHUNKS):
        to_far(c).wait_send()
        relay(c).wait_send()
        swap_sum(c).wait_send()
        send_sum(c).wait_send()

    @pl.loop(0, HEADS)
    def _(h):
        @pl.when(jnp.logical_not(is_me(to_dp, to_seq + h)))
        def _():
            for t in range(3):
                inward(t, h, 0).wait_send()

        @pl.when(jnp.logical_not(is_me(from_dp, 2 * h + core)))
        def _():
            backward(h, 0).wait_send()


def shards(images, boxes, w_embed, pos_embed, gain_attn, w_qkv, w_attn_out, gain_mlp, w_up, w_down):
    smem = pl.BlockSpec(memory_space=pltpu.SMEM)
    vmem = pl.BlockSpec(memory_space=pltpu.VMEM)
    hbm = pl.BlockSpec(memory_space=pl.ANY)
    sem = pltpu.SemaphoreType.DMA
    V = pltpu.VMEM
    out = pl.pallas_call(
        layer_kernel,
        out_shape=jax.ShapeDtypeStruct((TOK, WIDTH), BF16),
        in_specs=[smem, hbm, hbm, hbm, vmem, hbm, hbm, vmem, hbm, hbm],
        out_specs=vmem,
        scratch_shapes=[
            V((96, 1024), BF16), V((588, WIDTH), BF16), V((TOK, WIDTH), BF16), V((WIDTH, 3 * WIDTH), BF16),
            V((WIDTH, WIDTH), BF16), V((WIDTH, WIDTH), BF16), V((WIDTH, WIDTH), BF16), sem((9,)),
            V((1024, 1024), BF16), V((96, 1024), F32), V((SEQ, 32, 128), BF16), V((SEQ, 32, 128), BF16),
            V((1024, 1024), BF16), V((SEQ, 2, 16, 128), BF16), V((SEQ, 2, 16, 128), BF16),
            V((1024, 128), F32), V((TOK, OUT), BF16), V((OUT, WIDTH), BF16), V((TOK, WIDTH), F32),
            sem((SEQ,)), sem((SEQ,)), sem((SEQ,)), sem((SEQ,)),
            V((3, WIDTH, TOK), BF16), V((3, 96, 2048), BF16), V((2, 96, 2048), BF16), V((2048, 96), F32),
            V((2048, 128), F32), V((16, HEAD, TOK), BF16), V((WIDTH, TOK), BF16),
            sem((3, 16)), sem((3, 16)), sem((2,)), sem((2,)), sem((16,)), sem((16,)),
            V((TOK, WIDTH), BF16), V((TOK, WIDTH), BF16), V((TOK, WIDTH), BF16), V((TOK, WIDTH), BF16),
            V((TOK, WIDTH), F32), V((TOK, WIDTH), BF16), V((TOK, WIDTH), BF16), V((TOK, WIDTH), BF16),
            V((TOK, WIDTH), BF16), V((TOK, WIDTH), BF16), V((TOK, WIDTH), BF16),
            sem, sem, sem((CHUNKS,)), sem((CHUNKS,)), sem((CHUNKS,)), sem((CHUNKS,)), sem, sem,
            sem((CHUNKS,)), sem((CHUNKS,)), sem((CHUNKS,)), sem((CHUNKS,)),
        ],
        compiler_params=pltpu.CompilerParams(
            collective_id=0, has_side_effects=True, vmem_limit_bytes=60 * 1024 * 1024),
        name="layer",
    )(boxes, images, w_embed, pos_embed, gain_attn[None], w_qkv, w_attn_out, gain_mlp[None], w_up, w_down)
    return out[None]


def solution(mesh):
    return jax.shard_map(
        shards,
        mesh=mesh,
        in_specs=(
            P("dp", None, "seq", None), P(), P(), P("seq", None), P(), P(), P(), P(),
            P(None, "dp"), P("dp", None),
        ),
        out_specs=P("dp", "seq", None),
        check_vma=False,
    )
```

```python
import math

import jax
import jax.numpy as jnp
from jax import lax
from jax.experimental import pallas as pl
from jax.experimental.pallas import tpu as pltpu
from jax.sharding import PartitionSpec as P

HEADS = 16
HEAD = 80
PATCH = 14
OUT = 896
SEQ = 32
TOK = 128
WIDTH = 1280
MESH = pl.DeviceIdType.MESH
F32 = jnp.float32
BF16 = jnp.bfloat16


def taps(o, valid, first, length):
    numer = ((2 * o + 1) * length - OUT).astype(F32)
    lower = jnp.floor(numer * (1.0 / (2 * OUT)))
    remain = numer - lower * (2.0 * OUT)
    lower = jnp.where(remain < 0, lower - 1.0, jnp.where(remain >= 2.0 * OUT, lower + 1.0, lower))
    remain = numer - lower * (2.0 * OUT)
    lower = jnp.where(numer < 0, 0.0, lower).astype(jnp.int32)
    share = jnp.where(numer < 0, 0.0, remain) * (1.0 / (2 * OUT))
    upper = jnp.minimum(lower + 1, length - 1)
    near = jnp.where(valid, first + lower, -1)
    far = jnp.where(valid, first + upper, -1)
    return near, far, share


def layer_norm(values, gain):
    center = values - jnp.mean(values, axis=-1, keepdims=True)
    spread = jnp.mean(center * center, axis=-1, keepdims=True)
    return (center * lax.rsqrt(spread + 1e-06) * gain).astype(BF16)


def gelu(x):
    return 0.5 * x * (1.0 + lax.erf(x * (1.0 / math.sqrt(2.0))))


QB = 1024
KB = 512
CHUNKS = 2
ROWS = TOK // CHUNKS


def layer_kernel(
    boxes, images, w_embed, pos_embed, gain_attn, w_qkv, w_out, gain_mlp, w_up, w_down, result,
    img, emb, pos, qkv, outw, upw, downw, load,
    wcol, cmat, send1, recv1, wrow, send2, recv2, wide, tokens, embw, embedded, s1, r1, s2, r2,
    flat, mine, theirs, acc, peak, back, heads, s_in, r_in, s_swap, r_swap, s_back, r_back,
    normed, far_tok, total, giveback, fromfar, upw2, downw2, s_far, r_far, s_gb, r_gb, s_w, r_w,
):
    dp, me = lax.axis_index("dp"), lax.axis_index("seq")
    core, base = lax.rem(dp, 2), dp - lax.rem(dp, 2)
    half, slot = lax.rem(me, 2), me // 2
    image, head = me // 16, lax.rem(me, 16)
    to_dp, to_seq = base + half, core * 16
    from_dp = base + image
    sibling = (base + 1 - core, me)
    partner = (2 - base + core, me + 1 - 2 * half)

    def is_me(d, s):
        return jnp.logical_and(d == dp, s == me)

    loads = [
        pltpu.make_async_copy(a, b, load.at[i])
        for i, (a, b) in enumerate((
            (images.at[0, 0], img.at[pl.ds(0, 32)]), (images.at[0, 1], img.at[pl.ds(32, 32)]),
            (images.at[0, 2], img.at[pl.ds(64, 32)]), (w_embed, emb), (pos_embed, pos), (w_qkv, qkv),
            (w_out, outw), (w_up, upw), (w_down, downw)))
    ]
    for one in loads[:5]:
        one.start()

    barrier = pltpu.get_barrier_semaphore()

    def greet(d, s):
        pl.semaphore_signal(barrier, inc=1, device_id=(d, s), device_id_type=MESH)

    @pl.loop(1, SEQ)
    def _(k):
        greet(dp, lax.rem(me + k, SEQ))

    @pl.loop(0, HEADS)
    def _(h):
        @pl.when(jnp.logical_not(is_me(to_dp, to_seq + h)))
        def _():
            greet(to_dp, to_seq + h)

        @pl.when(jnp.logical_not(is_me(from_dp, 2 * h + core)))
        def _():
            greet(from_dp, 2 * h + core)

    greet(*sibling)
    greet(*partner)

    def remote(src, dst, s, r, device):
        return pltpu.make_async_remote_copy(
            src_ref=src, dst_ref=dst, send_sem=s, recv_sem=r, device_id=device, device_id_type=MESH)

    other = [remote(w_up, upw2, s_w.at[0], r_w.at[0], sibling), remote(w_down, downw2, s_w.at[1], r_w.at[1], sibling)]

    top, left, height, width = boxes[dp, 0], boxes[dp, 1], boxes[dp, 2], boxes[dp, 3]

    @pl.loop(0, 8)
    def _(t):
        lane = lax.broadcasted_iota(jnp.int32, (8, 128), 1)
        part, d4, j = lane // 64, (lane % 64) // 16, lane % 16
        o = (t * 4 + d4) * 28 + part * 14 + j
        near, far, share = taps(o, j < 14, left, width)
        near, far, share = near[:1], far[:1], share[:1]
        row = lax.broadcasted_iota(jnp.int32, (1024, 128), 0)
        w = jnp.where(row == near, 1.0 - share, 0.0) + jnp.where(row == far, share, 0.0)
        wcol[:, pl.ds(pl.multiple_of(t * 128, 128), 128)] = w.astype(BF16)

    for one in loads[:3]:
        one.wait()
    cmat[...] = jnp.dot(img[...], wcol[...], preferred_element_type=F32)

    @pl.loop(0, 8)
    def _(t):
        cols = pl.ds(pl.multiple_of(t * 128, 128), 128)
        lane = lax.broadcasted_iota(jnp.int32, (32, 128), 1)
        group = (lane % 64) // 16
        parts = [cmat[32 * ch : 32 * ch + 32, cols] for ch in range(3)]
        for d4 in range(4):
            chunk = jnp.zeros((32, 128), F32)
            for ch in range(3):
                shift = (16 * (ch - d4)) % 128
                moved = parts[ch] if shift == 0 else pltpu.roll(parts[ch], shift, 1)
                chunk = jnp.where(group == ch, moved, chunk)
            send1[t * 4 + d4] = chunk.astype(BF16)

    def first(dst, src):
        return pltpu.make_async_remote_copy(
            src_ref=send1.at[dst], dst_ref=recv1.at[src], send_sem=s1.at[dst], recv_sem=r1.at[src],
            device_id=(dp, dst), device_id_type=MESH)

    def second(dst, src):
        return pltpu.make_async_remote_copy(
            src_ref=send2.at[dst], dst_ref=recv2.at[src], send_sem=s2.at[dst], recv_sem=r2.at[src],
            device_id=(dp, dst), device_id_type=MESH)

    self_head = jnp.logical_and(half == core, core == image)
    pl.semaphore_wait(barrier, SEQ - 1 + 2 + jnp.where(self_head, 2 * 15, 2 * 16))

    @pl.loop(1, SEQ)
    def _(k):
        first(lax.rem(me + k, SEQ), me).start()

    loads[5].start()
    recv1[me] = send1[me]

    @pl.loop(0, 8)
    def _(t):
        row = lax.broadcasted_iota(jnp.int32, (128, 128), 0) + t * 128
        odd, d, kt, a2 = row // 512, (row % 512) // 16, (row % 16) // 2, row % 2
        o = (2 * d + a2) * 14 + 2 * kt + odd
        near, far, share = taps(o, kt < 7, top, height)
        rows = pl.ds(pl.multiple_of(t * 128, 128), 128)
        for c in range(8):
            col = lax.broadcasted_iota(jnp.int32, (128, 128), 1) + c * 128
            w = jnp.where(col == near, 1.0 - share, 0.0) + jnp.where(col == far, share, 0.0)
            wrow[rows, c * 128 : c * 128 + 128] = w.astype(BF16)

    @pl.loop(1, SEQ)
    def _(k):
        first(me, lax.rem(me + k, SEQ)).wait_recv()

    x = recv1[...].reshape(1024, 128)
    even = jnp.dot(wrow[:512], x, preferred_element_type=F32)
    odd = jnp.dot(wrow[512:], x, preferred_element_type=F32)
    low = lax.broadcasted_iota(jnp.int32, (512, 128), 1) < 64
    send2[:, 0] = jnp.where(low, even, pltpu.roll(odd, 64, 1)).astype(BF16).reshape(32, 16, 128)
    send2[:, 1] = jnp.where(low, pltpu.roll(even, 64, 1), odd).astype(BF16).reshape(32, 16, 128)

    @pl.loop(1, SEQ)
    def _(k):
        second(lax.rem(me + k, SEQ), me).start()

    recv2[me] = send2[me]

    for one in loads[3:5]:
        one.wait()

    @pl.loop(0, 7)
    def _(t):
        rho = lax.broadcasted_iota(jnp.int32, (128, 588), 0) + t * 128
        i, ch, j = rho // 64, (rho % 64) // 16, rho % 16
        origin = jnp.where(jnp.logical_and(ch < 3, j < 14), ch * 196 + i * 14 + j, -1)
        kappa = lax.broadcasted_iota(jnp.int32, (128, 588), 1)
        pick = jnp.where(origin == kappa, 1.0, 0.0).astype(BF16)
        rows = pl.ds(pl.multiple_of(t * 128, 128), 128)
        embw[rows, :] = jnp.dot(pick, emb[...], preferred_element_type=F32).astype(BF16)

    mine[0, HEAD:, :] = jnp.zeros((16, 2048), BF16)
    mine[1, HEAD:, :] = jnp.zeros((16, 2048), BF16)
    mine[2, HEAD:, :] = jnp.ones((16, 2048), BF16)

    @pl.loop(1, SEQ)
    def _(k):
        first(lax.rem(me + k, SEQ), me).wait_send()
        second(me, lax.rem(me + k, SEQ)).wait_recv()

    wide[...] = recv2[...].reshape(1024, 128).astype(F32)
    for kt in range(7):
        for a2 in range(2):
            piece = wide[pl.ds(kt * 2 + a2, 64, stride=16), :]
            tokens[a2 * 64 : a2 * 64 + 64, kt * 128 : kt * 128 + 128] = piece.astype(BF16)

    embedded[...] = jnp.dot(tokens[...], embw[...], preferred_element_type=F32) + pos[...].astype(F32)
    normed[...] = layer_norm(embedded[...], gain_attn[...].reshape(1, WIDTH))

    def head_rows(h):
        return pl.ds(pl.multiple_of(h * HEAD, 16), HEAD)

    def lanes(i):
        return pl.ds(pl.multiple_of(i * TOK, TOK), TOK)

    def inward(t, h, i):
        return pltpu.make_async_remote_copy(
            src_ref=flat.at[t, head_rows(h), :], dst_ref=mine.at[t, pl.ds(0, HEAD), lanes(i)],
            send_sem=s_in.at[t, h], recv_sem=r_in.at[t, i],
            device_id=(to_dp, to_seq + h), device_id_type=MESH)

    def backward(i, h):
        return pltpu.make_async_remote_copy(
            src_ref=back.at[i], dst_ref=heads.at[head_rows(h), :],
            send_sem=s_back.at[i], recv_sem=r_back.at[h],
            device_id=(from_dp, 2 * i + core), device_id_type=MESH)

    def turn(k):
        return lax.rem(slot // 4 + k // 4, 4) * 4 + lax.rem(slot + k, 4)

    def post(ts, first_k, last_k):
        @pl.loop(first_k, last_k)
        def _(k):
            h = turn(k)

            @pl.when(is_me(to_dp, to_seq + h))
            def _():
                for t in ts:
                    pltpu.make_async_copy(
                        flat.at[t, head_rows(h), :], mine.at[t, pl.ds(0, HEAD), lanes(slot)],
                        r_in.at[t, slot]).start()

            @pl.when(jnp.logical_not(is_me(to_dp, to_seq + h)))
            def _():
                for t in ts:
                    inward(t, h, slot).start()

    def posted(ts, first_k, last_k):
        @pl.loop(first_k, last_k)
        def _(k):
            h = turn(k)

            @pl.when(jnp.logical_not(is_me(to_dp, to_seq + h)))
            def _():
                for t in ts:
                    inward(t, h, slot).wait_send()

    def project(t, scale):
        proj = jnp.dot(normed[...], qkv[:, t * WIDTH : (t + 1) * WIDTH], preferred_element_type=F32)
        if scale is not None:
            proj = proj * scale
        for j in range(10):
            flat[t, j * 128 : j * 128 + 128, :] = proj[:, j * 128 : j * 128 + 128].T.astype(BF16)

    loads[5].wait()
    project(0, math.log2(math.e) / math.sqrt(HEAD))
    post((0,), 0, 16)
    project(1, None)
    project(2, None)
    post((1, 2), 0, 4)

    @pl.loop(1, SEQ)
    def _(k):
        second(lax.rem(me + k, SEQ), me).wait_send()

    for one in loads[6:]:
        one.start()
    for one in other:
        one.start()
    posted((0,), 0, 16)
    post((1, 2), 4, 8)

    def keys_of(g):
        return pl.ds(pl.multiple_of(g * KB, KB), KB)

    def swap(g):
        return pltpu.make_async_remote_copy(
            src_ref=mine.at[pl.ds(1, 2), :, keys_of(g)], dst_ref=theirs.at[:, :, keys_of(g)],
            send_sem=s_swap.at[g], recv_sem=r_swap.at[g], device_id=sibling, device_id_type=MESH)

    @pl.loop(0, HEADS)
    def _(i):
        inward(0, 0, i).wait_recv()

    peak[...] = jnp.full((8, 2048), -jnp.inf, F32)
    acc[...] = jnp.zeros((96, 2048), F32)

    def group(step):
        return lax.rem(head // 4 + 4 - step, 4)

    def take(keys, values, here):
        rows = keys.astype(F32).T.astype(BF16)
        s = jnp.dot(rows, mine[0, :, here], preferred_element_type=F32)
        old = peak[:1, here]
        new = jnp.maximum(old, jnp.max(s, axis=0, keepdims=True))
        p = jnp.exp2(s - new).astype(BF16)
        return new, acc[:, here] * jnp.exp2(old - new) + jnp.dot(values, p, preferred_element_type=F32)

    def absorb(keys, values):
        new, sums = take(keys, values, slice(0, 2048))
        acc[...] = sums
        peak[...] = jnp.broadcast_to(new, (8, 2048))

    @pl.loop(0, 4)
    def _(step):
        g = group(step)

        @pl.when(step < 2)
        def _():
            posted((1, 2), step * 4, step * 4 + 4)
            post((1, 2), step * 4 + 8, step * 4 + 12)

        for j in range(4):
            for t in (1, 2):
                inward(t, 0, g * 4 + j).wait_recv()
        swap(g).start()
        absorb(mine[1, :, keys_of(g)], mine[2, :, keys_of(g)])

        @pl.when(step > 0)
        def _():
            earlier = group(step - 1)
            swap(earlier).wait_recv()
            absorb(theirs[0, :, keys_of(earlier)], theirs[1, :, keys_of(earlier)])

    last = group(3)
    swap(last).wait_recv()
    for step in range(2048 // QB):
        b = lax.rem(step + head, 2048 // QB)
        _, o = take(
            theirs[0, :, keys_of(last)], theirs[1, :, keys_of(last)],
            pl.ds(pl.multiple_of(b * QB, QB), QB))
        o = (o[:HEAD] / o[HEAD : HEAD + 1]).astype(BF16)
        for j in range(QB // TOK):
            back[b * (QB // TOK) + j] = o[:, j * TOK : j * TOK + TOK]

        @pl.loop(0, QB // TOK)
        def _(j):
            i = b * (QB // TOK) + lax.rem(j + head, QB // TOK)

            @pl.when(is_me(from_dp, 2 * i + core))
            def _():
                pltpu.make_async_copy(back.at[i], heads.at[head_rows(head), :], r_back.at[head]).start()

            @pl.when(jnp.logical_not(is_me(from_dp, 2 * i + core)))
            def _():
                backward(i, head).start()

    for one in loads[6:]:
        one.wait()

    @pl.loop(0, HEADS)
    def _(h):
        backward(0, h).wait_recv()

    attended = jnp.concatenate(
        [heads[j * 128 : j * 128 + 128, :].astype(F32).T.astype(BF16) for j in range(10)], axis=1)
    middle = embedded[...] + jnp.dot(attended, outw[...], preferred_element_type=F32)
    embedded[...] = middle
    normed[...] = layer_norm(middle, gain_mlp[...].reshape(1, WIDTH))

    def chunk(c):
        return pl.ds(c * ROWS, ROWS)

    def to_far(c):
        return remote(normed.at[chunk(c)], far_tok.at[chunk(c)], s_far.at[c], r_far.at[c], partner)

    def send_sum(c):
        return remote(giveback.at[chunk(c)], fromfar.at[chunk(c)], s_gb.at[c], r_gb.at[c], partner)

    def mlp(x):
        sums = None
        for up, down in ((upw, downw), (upw2, downw2)):
            hidden = gelu(jnp.dot(x, up[...], preferred_element_type=F32)).astype(BF16)
            part = jnp.dot(hidden, down[...], preferred_element_type=F32)
            sums = part if sums is None else sums + part
        return sums

    for c in range(CHUNKS):
        to_far(c).start()
    for one in other:
        one.wait_recv()
    total[...] = embedded[...] + mlp(normed[...])
    for c in range(CHUNKS):
        to_far(c).wait_recv()
        giveback[chunk(c), :] = mlp(far_tok[chunk(c), :]).astype(BF16)
        send_sum(c).start()
    for c in range(CHUNKS):
        send_sum(c).wait_recv()
        result[chunk(c), :] = (total[chunk(c), :] + fromfar[chunk(c), :].astype(F32)).astype(BF16)

    posted((1, 2), 8, 16)
    for one in other:
        one.wait_send()
    for g in range(4):
        swap(g).wait_send()
    for c in range(CHUNKS):
        to_far(c).wait_send()
        send_sum(c).wait_send()

    @pl.loop(0, HEADS)
    def _(h):
        @pl.when(jnp.logical_not(is_me(from_dp, 2 * h + core)))
        def _():
            backward(h, 0).wait_send()


def shards(images, boxes, w_embed, pos_embed, gain_attn, w_qkv, w_attn_out, gain_mlp, w_up, w_down):
    smem = pl.BlockSpec(memory_space=pltpu.SMEM)
    vmem = pl.BlockSpec(memory_space=pltpu.VMEM)
    hbm = pl.BlockSpec(memory_space=pl.ANY)
    sem = pltpu.SemaphoreType.DMA
    V = pltpu.VMEM
    out = pl.pallas_call(
        layer_kernel,
        out_shape=jax.ShapeDtypeStruct((TOK, WIDTH), BF16),
        in_specs=[smem, hbm, hbm, hbm, vmem, hbm, hbm, vmem, hbm, hbm],
        out_specs=vmem,
        scratch_shapes=[
            V((96, 1024), BF16), V((588, WIDTH), BF16), V((TOK, WIDTH), BF16), V((WIDTH, 3 * WIDTH), BF16),
            V((WIDTH, WIDTH), BF16), V((WIDTH, WIDTH), BF16), V((WIDTH, WIDTH), BF16), sem((9,)),
            V((1024, 1024), BF16), V((96, 1024), F32), V((SEQ, 32, 128), BF16), V((SEQ, 32, 128), BF16),
            V((1024, 1024), BF16), V((SEQ, 2, 16, 128), BF16), V((SEQ, 2, 16, 128), BF16),
            V((1024, 128), F32), V((TOK, OUT), BF16), V((OUT, WIDTH), BF16), V((TOK, WIDTH), F32),
            sem((SEQ,)), sem((SEQ,)), sem((SEQ,)), sem((SEQ,)),
            V((3, WIDTH, TOK), BF16), V((3, 96, 2048), BF16), V((2, 96, 2048), BF16),
            V((96, 2048), F32), V((8, 2048), F32), V((16, HEAD, TOK), BF16), V((WIDTH, TOK), BF16),
            sem((3, 16)), sem((3, 16)), sem((4,)), sem((4,)), sem((16,)), sem((16,)),
            V((TOK, WIDTH), BF16), V((TOK, WIDTH), BF16), V((TOK, WIDTH), F32), V((TOK, WIDTH), BF16),
            V((TOK, WIDTH), BF16), V((WIDTH, WIDTH), BF16), V((WIDTH, WIDTH), BF16),
            sem((CHUNKS,)), sem((CHUNKS,)), sem((CHUNKS,)), sem((CHUNKS,)), sem((2,)), sem((2,)),
        ],
        compiler_params=pltpu.CompilerParams(
            collective_id=0, has_side_effects=True, vmem_limit_bytes=60 * 1024 * 1024),
        name="layer",
    )(boxes, images, w_embed, pos_embed, gain_attn, w_qkv, w_attn_out, gain_mlp, w_up, w_down)
    return out[None]


def solution(mesh):
    return jax.shard_map(
        shards,
        mesh=mesh,
        in_specs=(
            P("dp", None, "seq", None), P(), P(), P("seq", None), P(), P(), P(), P(),
            P(None, "dp"), P("dp", None),
        ),
        out_specs=P("dp", "seq", None),
        check_vma=False,
    )
```

```python
import math

import jax
import jax.numpy as jnp
from jax import lax
from jax.experimental import pallas as pl
from jax.experimental.pallas import tpu as pltpu
from jax.sharding import PartitionSpec as P

HEADS = 16
HEAD = 80
PATCH = 14
OUT = 896
SEQ = 32
TOK = 128
WIDTH = 1280
MESH = pl.DeviceIdType.MESH
F32 = jnp.float32
BF16 = jnp.bfloat16


def taps(o, valid, first, length):
    numer = ((2 * o + 1) * length - OUT).astype(F32)
    lower = jnp.floor(numer * (1.0 / (2 * OUT)))
    remain = numer - lower * (2.0 * OUT)
    lower = jnp.where(remain < 0, lower - 1.0, jnp.where(remain >= 2.0 * OUT, lower + 1.0, lower))
    remain = numer - lower * (2.0 * OUT)
    lower = jnp.where(numer < 0, 0.0, lower).astype(jnp.int32)
    share = jnp.where(numer < 0, 0.0, remain) * (1.0 / (2 * OUT))
    upper = jnp.minimum(lower + 1, length - 1)
    near = jnp.where(valid, first + lower, -1)
    far = jnp.where(valid, first + upper, -1)
    return near, far, share


def layer_norm(values, gain):
    center = values - jnp.mean(values, axis=-1, keepdims=True)
    spread = jnp.mean(center * center, axis=-1, keepdims=True)
    return (center * lax.rsqrt(spread + 1e-06) * gain).astype(BF16)


def gelu(x):
    return 0.5 * x * (1.0 + lax.erf(x * (1.0 / math.sqrt(2.0))))


QB = 1024
KB = 512
CHUNKS = 2
ROWS = TOK // CHUNKS


def layer_kernel(
    boxes_in, images, w_embed, pos_embed, gain_in, w_qkv, w_out, gain2_in, w_up, w_down, result,
    boxes, gain_attn, gain_mlp, small, img, emb, pos, qkv, outw, upw, downw, load,
    wcol, cmat, send1, recv1, wrow, send2, recv2, wide, tokens, embw, embedded, s1, r1, s2, r2,
    flat, mine, theirs, acc, peak, back, heads, s_in, r_in, s_swap, r_swap, s_back, r_back,
    normed, far_tok, total, giveback, fromfar, upw2, downw2, s_far, r_far, s_gb, r_gb, s_w, r_w,
):
    dp, me = lax.axis_index("dp"), lax.axis_index("seq")
    core, base = lax.rem(dp, 2), dp - lax.rem(dp, 2)
    half, slot = lax.rem(me, 2), me // 2
    image, head = me // 16, lax.rem(me, 16)
    to_dp, to_seq = base + half, core * 16
    from_dp = base + image
    sibling = (base + 1 - core, me)
    partner = (2 - base + core, me + 1 - 2 * half)

    def is_me(d, s):
        return jnp.logical_and(d == dp, s == me)

    barrier = pltpu.get_barrier_semaphore()

    def greet(d, s):
        pl.semaphore_signal(barrier, inc=1, device_id=(d, s), device_id_type=MESH)

    @pl.loop(1, SEQ)
    def _(k):
        greet(dp, lax.rem(me + k, SEQ))

    @pl.loop(0, HEADS)
    def _(h):
        @pl.when(jnp.logical_not(is_me(to_dp, to_seq + h)))
        def _():
            greet(to_dp, to_seq + h)

        @pl.when(jnp.logical_not(is_me(from_dp, 2 * h + core)))
        def _():
            greet(from_dp, 2 * h + core)

    greet(*sibling)
    greet(*partner)

    smalls = [
        pltpu.make_async_copy(a, b, small.at[i])
        for i, (a, b) in enumerate(((boxes_in, boxes), (gain_in, gain_attn), (gain2_in, gain_mlp)))
    ]
    for one in smalls:
        one.start()

    loads = [
        pltpu.make_async_copy(a, b, load.at[i])
        for i, (a, b) in enumerate((
            (images.at[0, 0], img.at[pl.ds(0, 32)]), (images.at[0, 1], img.at[pl.ds(32, 32)]),
            (images.at[0, 2], img.at[pl.ds(64, 32)]), (w_embed, emb), (pos_embed, pos), (w_qkv, qkv),
            (w_out, outw), (w_up, upw), (w_down, downw)))
    ]
    for one in loads[:5]:
        one.start()

    def remote(src, dst, s, r, device):
        return pltpu.make_async_remote_copy(
            src_ref=src, dst_ref=dst, send_sem=s, recv_sem=r, device_id=device, device_id_type=MESH)

    other = [remote(w_up, upw2, s_w.at[0], r_w.at[0], sibling), remote(w_down, downw2, s_w.at[1], r_w.at[1], sibling)]

    for one in smalls:
        one.wait()
    top, left, height, width = boxes[dp, 0], boxes[dp, 1], boxes[dp, 2], boxes[dp, 3]

    @pl.loop(0, 8)
    def _(t):
        lane = lax.broadcasted_iota(jnp.int32, (8, 128), 1)
        part, d4, j = lane // 64, (lane % 64) // 16, lane % 16
        o = (t * 4 + d4) * 28 + part * 14 + j
        near, far, share = taps(o, j < 14, left, width)
        near, far, share = near[:1], far[:1], share[:1]
        row = lax.broadcasted_iota(jnp.int32, (1024, 128), 0)
        w = jnp.where(row == near, 1.0 - share, 0.0) + jnp.where(row == far, share, 0.0)
        wcol[:, pl.ds(pl.multiple_of(t * 128, 128), 128)] = w.astype(BF16)

    for one in loads[:3]:
        one.wait()
    cmat[...] = jnp.dot(img[...], wcol[...], preferred_element_type=F32)

    @pl.loop(0, 8)
    def _(t):
        cols = pl.ds(pl.multiple_of(t * 128, 128), 128)
        lane = lax.broadcasted_iota(jnp.int32, (32, 128), 1)
        group = (lane % 64) // 16
        parts = [cmat[32 * ch : 32 * ch + 32, cols] for ch in range(3)]
        for d4 in range(4):
            chunk = jnp.zeros((32, 128), F32)
            for ch in range(3):
                shift = (16 * (ch - d4)) % 128
                moved = parts[ch] if shift == 0 else pltpu.roll(parts[ch], shift, 1)
                chunk = jnp.where(group == ch, moved, chunk)
            send1[t * 4 + d4] = chunk.astype(BF16)

    def first(dst, src):
        return pltpu.make_async_remote_copy(
            src_ref=send1.at[dst], dst_ref=recv1.at[src], send_sem=s1.at[dst], recv_sem=r1.at[src],
            device_id=(dp, dst), device_id_type=MESH)

    def second(dst, src):
        return pltpu.make_async_remote_copy(
            src_ref=send2.at[dst], dst_ref=recv2.at[src], send_sem=s2.at[dst], recv_sem=r2.at[src],
            device_id=(dp, dst), device_id_type=MESH)

    self_head = jnp.logical_and(half == core, core == image)
    pl.semaphore_wait(barrier, SEQ - 1 + 2 + jnp.where(self_head, 2 * 15, 2 * 16))

    @pl.loop(1, SEQ)
    def _(k):
        first(lax.rem(me + k, SEQ), me).start()

    loads[5].start()
    recv1[me] = send1[me]

    @pl.loop(0, 8)
    def _(t):
        row = lax.broadcasted_iota(jnp.int32, (128, 128), 0) + t * 128
        odd, d, kt, a2 = row // 512, (row % 512) // 16, (row % 16) // 2, row % 2
        o = (2 * d + a2) * 14 + 2 * kt + odd
        near, far, share = taps(o, kt < 7, top, height)
        rows = pl.ds(pl.multiple_of(t * 128, 128), 128)
        for c in range(8):
            col = lax.broadcasted_iota(jnp.int32, (128, 128), 1) + c * 128
            w = jnp.where(col == near, 1.0 - share, 0.0) + jnp.where(col == far, share, 0.0)
            wrow[rows, c * 128 : c * 128 + 128] = w.astype(BF16)

    @pl.loop(1, SEQ)
    def _(k):
        first(me, lax.rem(me + k, SEQ)).wait_recv()

    x = recv1[...].reshape(1024, 128)
    even = jnp.dot(wrow[:512], x, preferred_element_type=F32)
    odd = jnp.dot(wrow[512:], x, preferred_element_type=F32)
    low = lax.broadcasted_iota(jnp.int32, (512, 128), 1) < 64
    send2[:, 0] = jnp.where(low, even, pltpu.roll(odd, 64, 1)).astype(BF16).reshape(32, 16, 128)
    send2[:, 1] = jnp.where(low, pltpu.roll(even, 64, 1), odd).astype(BF16).reshape(32, 16, 128)

    @pl.loop(1, SEQ)
    def _(k):
        second(lax.rem(me + k, SEQ), me).start()

    recv2[me] = send2[me]

    for one in loads[3:5]:
        one.wait()

    @pl.loop(0, 7)
    def _(t):
        rho = lax.broadcasted_iota(jnp.int32, (128, 588), 0) + t * 128
        i, ch, j = rho // 64, (rho % 64) // 16, rho % 16
        origin = jnp.where(jnp.logical_and(ch < 3, j < 14), ch * 196 + i * 14 + j, -1)
        kappa = lax.broadcasted_iota(jnp.int32, (128, 588), 1)
        pick = jnp.where(origin == kappa, 1.0, 0.0).astype(BF16)
        rows = pl.ds(pl.multiple_of(t * 128, 128), 128)
        embw[rows, :] = jnp.dot(pick, emb[...], preferred_element_type=F32).astype(BF16)

    mine[0, HEAD:, :] = jnp.zeros((16, 2048), BF16)
    mine[1, HEAD:, :] = jnp.zeros((16, 2048), BF16)
    mine[2, HEAD:, :] = jnp.ones((16, 2048), BF16)

    @pl.loop(1, SEQ)
    def _(k):
        first(lax.rem(me + k, SEQ), me).wait_send()
        second(me, lax.rem(me + k, SEQ)).wait_recv()

    wide[...] = recv2[...].reshape(1024, 128).astype(F32)
    for kt in range(7):
        for a2 in range(2):
            piece = wide[pl.ds(kt * 2 + a2, 64, stride=16), :]
            tokens[a2 * 64 : a2 * 64 + 64, kt * 128 : kt * 128 + 128] = piece.astype(BF16)

    embedded[...] = jnp.dot(tokens[...], embw[...], preferred_element_type=F32) + pos[...].astype(F32)
    normed[...] = layer_norm(embedded[...], gain_attn[...].reshape(1, WIDTH))

    def head_rows(h):
        return pl.ds(pl.multiple_of(h * HEAD, 16), HEAD)

    def lanes(i):
        return pl.ds(pl.multiple_of(i * TOK, TOK), TOK)

    def span(t):
        return pl.ds(t, 1 + t)

    def inward(t, h, i):
        return pltpu.make_async_remote_copy(
            src_ref=flat.at[span(t), head_rows(h), :], dst_ref=mine.at[span(t), pl.ds(0, HEAD), lanes(i)],
            send_sem=s_in.at[t, h], recv_sem=r_in.at[t, i],
            device_id=(to_dp, to_seq + h), device_id_type=MESH)

    def backward(i, h):
        return pltpu.make_async_remote_copy(
            src_ref=back.at[i], dst_ref=heads.at[head_rows(h), :],
            send_sem=s_back.at[i], recv_sem=r_back.at[h],
            device_id=(from_dp, 2 * i + core), device_id_type=MESH)

    def turn(k):
        return lax.rem(slot // 4 + k // 4, 4) * 4 + lax.rem(slot + k, 4)

    def post(ts, first_k, last_k):
        @pl.loop(first_k, last_k)
        def _(k):
            h = turn(k)

            @pl.when(is_me(to_dp, to_seq + h))
            def _():
                for t in ts:
                    pltpu.make_async_copy(
                        flat.at[span(t), head_rows(h), :], mine.at[span(t), pl.ds(0, HEAD), lanes(slot)],
                        r_in.at[t, slot]).start()

            @pl.when(jnp.logical_not(is_me(to_dp, to_seq + h)))
            def _():
                for t in ts:
                    inward(t, h, slot).start()

    def posted(ts, first_k, last_k):
        @pl.loop(first_k, last_k)
        def _(k):
            h = turn(k)

            @pl.when(jnp.logical_not(is_me(to_dp, to_seq + h)))
            def _():
                for t in ts:
                    inward(t, h, slot).wait_send()

    def project(t, scale):
        proj = jnp.dot(normed[...], qkv[:, t * WIDTH : (t + 1) * WIDTH], preferred_element_type=F32)
        if scale is not None:
            proj = proj * scale
        for j in range(10):
            flat[t, j * 128 : j * 128 + 128, :] = proj[:, j * 128 : j * 128 + 128].T.astype(BF16)

    loads[5].wait()
    project(0, math.log2(math.e) / math.sqrt(HEAD))
    post((0,), 0, 16)
    project(1, None)
    project(2, None)
    post((1,), 0, 4)

    @pl.loop(1, SEQ)
    def _(k):
        second(lax.rem(me + k, SEQ), me).wait_send()

    for one in loads[6:]:
        one.start()
    for one in other:
        one.start()
    posted((0,), 0, 16)
    post((1,), 4, 8)

    def keys_of(g):
        return pl.ds(pl.multiple_of(g * KB, KB), KB)

    def swap(g):
        return pltpu.make_async_remote_copy(
            src_ref=mine.at[pl.ds(1, 2), :, keys_of(g)], dst_ref=theirs.at[:, :, keys_of(g)],
            send_sem=s_swap.at[g], recv_sem=r_swap.at[g], device_id=sibling, device_id_type=MESH)

    @pl.loop(0, HEADS)
    def _(i):
        inward(0, 0, i).wait_recv()

    peak[...] = jnp.full((8, 2048), -jnp.inf, F32)
    acc[...] = jnp.zeros((96, 2048), F32)

    def group(step):
        return lax.rem(head // 4 + 4 - step, 4)

    def take(keys, values, q, old, sums):
        rows = keys.astype(F32).T.astype(BF16)
        s = jnp.dot(rows, q, preferred_element_type=F32)
        new = jnp.maximum(old, jnp.max(s, axis=0, keepdims=True))
        p = jnp.exp2(s - new).astype(BF16)
        return new, sums * jnp.exp2(old - new) + jnp.dot(values, p, preferred_element_type=F32)

    def arrived(g):
        for j in range(4):
            inward(1, 0, g * 4 + j).wait_recv()
        swap(g).start()

    def keep(new, sums):
        acc[...] = sums
        peak[...] = jnp.broadcast_to(new, (8, 2048))

    posted((1,), 0, 4)
    post((1,), 8, 12)
    begin = group(0)
    arrived(begin)
    keep(*take(mine[1, :, keys_of(begin)], mine[2, :, keys_of(begin)], mine[0], peak[:1, :], acc[...]))

    @pl.loop(1, 4)
    def _(step):
        @pl.when(step == 1)
        def _():
            posted((1,), 4, 8)
            post((1,), 12, 16)

        g, earlier = group(step), group(step - 1)
        arrived(g)
        swap(earlier).wait_recv()
        keep(*take(
            jnp.concatenate([theirs[0, :, keys_of(earlier)], mine[1, :, keys_of(g)]], axis=1),
            jnp.concatenate([theirs[1, :, keys_of(earlier)], mine[2, :, keys_of(g)]], axis=1),
            mine[0], peak[:1, :], acc[...]))

    last = group(3)
    swap(last).wait_recv()
    for step in range(2048 // QB):
        b = lax.rem(step + head, 2048 // QB)
        here = pl.ds(pl.multiple_of(b * QB, QB), QB)
        _, o = take(
            theirs[0, :, keys_of(last)], theirs[1, :, keys_of(last)], mine[0, :, here], peak[:1, here],
            acc[:, here])
        o = (o[:HEAD] / o[HEAD : HEAD + 1]).astype(BF16)
        for j in range(QB // TOK):
            back[b * (QB // TOK) + j] = o[:, j * TOK : j * TOK + TOK]

        @pl.loop(0, QB // TOK)
        def _(j):
            i = b * (QB // TOK) + lax.rem(j + head, QB // TOK)

            @pl.when(is_me(from_dp, 2 * i + core))
            def _():
                pltpu.make_async_copy(back.at[i], heads.at[head_rows(head), :], r_back.at[head]).start()

            @pl.when(jnp.logical_not(is_me(from_dp, 2 * i + core)))
            def _():
                backward(i, head).start()

    for one in loads[6:]:
        one.wait()

    @pl.loop(0, HEADS)
    def _(h):
        backward(0, h).wait_recv()

    attended = jnp.concatenate(
        [heads[j * 128 : j * 128 + 128, :].astype(F32).T.astype(BF16) for j in range(10)], axis=1)
    middle = embedded[...] + jnp.dot(attended, outw[...], preferred_element_type=F32)
    embedded[...] = middle
    normed[...] = layer_norm(middle, gain_mlp[...].reshape(1, WIDTH))

    def chunk(c):
        return pl.ds(c * ROWS, ROWS)

    def to_far(c):
        return remote(normed.at[chunk(c)], far_tok.at[chunk(c)], s_far.at[c], r_far.at[c], partner)

    parts = (pl.ds(0, 768), pl.ds(768, 512))

    def send_sum(c, k):
        return remote(
            giveback.at[chunk(c), parts[k]], fromfar.at[chunk(c), parts[k]], s_gb.at[c, k], r_gb.at[c, k], partner)

    def hidden_of(x):
        return [gelu(jnp.dot(x, up[...], preferred_element_type=F32)).astype(BF16) for up in (upw, upw2)]

    def summed(hidden, part):
        return jnp.dot(hidden[0], downw[:, part], preferred_element_type=F32) + jnp.dot(
            hidden[1], downw2[:, part], preferred_element_type=F32)

    for c in range(CHUNKS):
        to_far(c).start()
    for one in other:
        one.wait_recv()
    total[...] = embedded[...] + summed(hidden_of(normed[...]), slice(None))
    for c in range(CHUNKS):
        to_far(c).wait_recv()
        hidden = hidden_of(far_tok[chunk(c), :])
        for k, part in enumerate(parts):
            giveback[chunk(c), part] = summed(hidden, part).astype(BF16)
            send_sum(c, k).start()
    for c in range(CHUNKS):
        for k in range(2):
            send_sum(c, k).wait_recv()
        result[chunk(c), :] = (total[chunk(c), :] + fromfar[chunk(c), :].astype(F32)).astype(BF16)

    posted((1,), 8, 16)
    for one in other:
        one.wait_send()
    for g in range(4):
        swap(g).wait_send()
    for c in range(CHUNKS):
        to_far(c).wait_send()
        for k in range(2):
            send_sum(c, k).wait_send()

    @pl.loop(0, HEADS)
    def _(h):
        @pl.when(jnp.logical_not(is_me(from_dp, 2 * h + core)))
        def _():
            backward(h, 0).wait_send()


def shards(images, boxes, w_embed, pos_embed, gain_attn, w_qkv, w_attn_out, gain_mlp, w_up, w_down):
    vmem = pl.BlockSpec(memory_space=pltpu.VMEM)
    hbm = pl.BlockSpec(memory_space=pl.ANY)
    sem = pltpu.SemaphoreType.DMA
    V = pltpu.VMEM
    out = pl.pallas_call(
        layer_kernel,
        out_shape=jax.ShapeDtypeStruct((TOK, WIDTH), BF16),
        in_specs=[hbm] * 10,
        out_specs=vmem,
        scratch_shapes=[
            pltpu.SMEM((4, 4), jnp.int32), V((WIDTH,), F32), V((WIDTH,), F32), sem((3,)),
            V((96, 1024), BF16), V((588, WIDTH), BF16), V((TOK, WIDTH), BF16), V((WIDTH, 3 * WIDTH), BF16),
            V((WIDTH, WIDTH), BF16), V((WIDTH, WIDTH), BF16), V((WIDTH, WIDTH), BF16), sem((9,)),
            V((1024, 1024), BF16), V((96, 1024), F32), V((SEQ, 32, 128), BF16), V((SEQ, 32, 128), BF16),
            V((1024, 1024), BF16), V((SEQ, 2, 16, 128), BF16), V((SEQ, 2, 16, 128), BF16),
            V((1024, 128), F32), V((TOK, OUT), BF16), V((OUT, WIDTH), BF16), V((TOK, WIDTH), F32),
            sem((SEQ,)), sem((SEQ,)), sem((SEQ,)), sem((SEQ,)),
            V((3, WIDTH, TOK), BF16), V((3, 96, 2048), BF16), V((2, 96, 2048), BF16),
            V((96, 2048), F32), V((8, 2048), F32), V((16, HEAD, TOK), BF16), V((WIDTH, TOK), BF16),
            sem((2, 16)), sem((2, 16)), sem((4,)), sem((4,)), sem((16,)), sem((16,)),
            V((TOK, WIDTH), BF16), V((TOK, WIDTH), BF16), V((TOK, WIDTH), F32), V((TOK, WIDTH), BF16),
            V((TOK, WIDTH), BF16), V((WIDTH, WIDTH), BF16), V((WIDTH, WIDTH), BF16),
            sem((CHUNKS,)), sem((CHUNKS,)), sem((CHUNKS, 2)), sem((CHUNKS, 2)), sem((2,)), sem((2,)),
        ],
        compiler_params=pltpu.CompilerParams(
            collective_id=0, has_side_effects=True, vmem_limit_bytes=60 * 1024 * 1024),
        name="layer",
    )(boxes, images, w_embed, pos_embed, gain_attn, w_qkv, w_attn_out, gain_mlp, w_up, w_down)
    return out[None]


def solution(mesh):
    return jax.shard_map(
        shards,
        mesh=mesh,
        in_specs=(
            P("dp", None, "seq", None), P(), P(), P("seq", None), P(), P(), P(), P(),
            P(None, "dp"), P("dp", None),
        ),
        out_specs=P("dp", "seq", None),
        check_vma=False,
    )
```

```python
import math

import jax
import jax.numpy as jnp
from jax import lax
from jax.experimental import pallas as pl
from jax.experimental.pallas import tpu as pltpu
from jax.sharding import PartitionSpec as P

HEADS = 16
HEAD = 80
PATCH = 14
OUT = 896
SEQ = 32
TOK = 128
WIDTH = 1280
MESH = pl.DeviceIdType.MESH
F32 = jnp.float32
BF16 = jnp.bfloat16


def taps(o, valid, first, length):
    numer = ((2 * o + 1) * length - OUT).astype(F32)
    lower = jnp.floor(numer * (1.0 / (2 * OUT)))
    remain = numer - lower * (2.0 * OUT)
    lower = jnp.where(remain < 0, lower - 1.0, jnp.where(remain >= 2.0 * OUT, lower + 1.0, lower))
    remain = numer - lower * (2.0 * OUT)
    lower = jnp.where(numer < 0, 0.0, lower).astype(jnp.int32)
    share = jnp.where(numer < 0, 0.0, remain) * (1.0 / (2 * OUT))
    upper = jnp.minimum(lower + 1, length - 1)
    near = jnp.where(valid, first + lower, -1)
    far = jnp.where(valid, first + upper, -1)
    return near, far, share


def layer_norm(values, gain):
    center = values - jnp.mean(values, axis=-1, keepdims=True)
    spread = jnp.mean(center * center, axis=-1, keepdims=True)
    return (center * lax.rsqrt(spread + 1e-06) * gain).astype(BF16)


def gelu(x):
    return 0.5 * x * (1.0 + lax.erf(x * (1.0 / math.sqrt(2.0))))


QB = 1024
KB = 512
CHUNKS = 2
ROWS = TOK // CHUNKS


def layer_kernel(
    boxes_in, images, w_embed, pos_embed, gain_in, w_qkv, w_out, gain2_in, w_up, w_down, result,
    boxes, gain_attn, gain_mlp, small, img, emb, pos, qkv, outw, upw, downw, load,
    wcol, cmat, send1, recv1, wrow, send2, recv2, wide, tokens, embw, embedded, s1, r1, s2, r2,
    flat, mine, theirs, acc, peak, back, heads, s_in, r_in, s_swap, r_swap, s_back, r_back,
    normed, far_tok, total, giveback, fromfar, upw2, downw2, s_far, r_far, s_gb, r_gb, s_w, r_w,
):
    dp, me = lax.axis_index("dp"), lax.axis_index("seq")
    core, base = lax.rem(dp, 2), dp - lax.rem(dp, 2)
    half, slot = lax.rem(me, 2), me // 2
    image, head = me // 16, lax.rem(me, 16)
    to_dp, to_seq = base + half, core * 16
    from_dp = base + image
    sibling = (base + 1 - core, me)
    partner = (2 - base + core, me + 1 - 2 * half)

    def is_me(d, s):
        return jnp.logical_and(d == dp, s == me)

    barrier = pltpu.get_barrier_semaphore()

    def greet(d, s):
        pl.semaphore_signal(barrier, inc=1, device_id=(d, s), device_id_type=MESH)

    @pl.loop(1, SEQ)
    def _(k):
        greet(dp, lax.rem(me + k, SEQ))

    @pl.loop(0, HEADS)
    def _(h):
        @pl.when(jnp.logical_not(is_me(to_dp, to_seq + h)))
        def _():
            greet(to_dp, to_seq + h)

        @pl.when(jnp.logical_not(is_me(from_dp, 2 * h + core)))
        def _():
            greet(from_dp, 2 * h + core)

    greet(*sibling)
    greet(*partner)

    smalls = [
        pltpu.make_async_copy(a, b, small.at[i])
        for i, (a, b) in enumerate(((boxes_in, boxes), (gain_in, gain_attn), (gain2_in, gain_mlp)))
    ]
    for one in smalls:
        one.start()

    loads = [
        pltpu.make_async_copy(a, b, load.at[i])
        for i, (a, b) in enumerate((
            (images.at[0, 0], img.at[pl.ds(0, 32)]), (images.at[0, 1], img.at[pl.ds(32, 32)]),
            (images.at[0, 2], img.at[pl.ds(64, 32)]), (w_embed, emb), (pos_embed, pos), (w_qkv, qkv),
            (w_out, outw), (w_up, upw), (w_down, downw)))
    ]
    for one in loads[:5]:
        one.start()

    def remote(src, dst, s, r, device):
        return pltpu.make_async_remote_copy(
            src_ref=src, dst_ref=dst, send_sem=s, recv_sem=r, device_id=device, device_id_type=MESH)

    other = [remote(w_up, upw2, s_w.at[0], r_w.at[0], sibling), remote(w_down, downw2, s_w.at[1], r_w.at[1], sibling)]

    for one in smalls:
        one.wait()
    top, left, height, width = boxes[dp, 0], boxes[dp, 1], boxes[dp, 2], boxes[dp, 3]

    @pl.loop(0, 8)
    def _(t):
        lane = lax.broadcasted_iota(jnp.int32, (8, 128), 1)
        part, d4, j = lane // 64, (lane % 64) // 16, lane % 16
        o = (t * 4 + d4) * 28 + part * 14 + j
        near, far, share = taps(o, j < 14, left, width)
        near, far, share = near[:1], far[:1], share[:1]
        row = lax.broadcasted_iota(jnp.int32, (1024, 128), 0)
        w = jnp.where(row == near, 1.0 - share, 0.0) + jnp.where(row == far, share, 0.0)
        wcol[:, pl.ds(pl.multiple_of(t * 128, 128), 128)] = w.astype(BF16)

    for one in loads[:3]:
        one.wait()
    cmat[...] = jnp.dot(img[...], wcol[...], preferred_element_type=F32)

    @pl.loop(0, 8)
    def _(t):
        cols = pl.ds(pl.multiple_of(t * 128, 128), 128)
        lane = lax.broadcasted_iota(jnp.int32, (32, 128), 1)
        group = (lane % 64) // 16
        parts = [cmat[32 * ch : 32 * ch + 32, cols] for ch in range(3)]
        for d4 in range(4):
            chunk = jnp.zeros((32, 128), F32)
            for ch in range(3):
                shift = (16 * (ch - d4)) % 128
                moved = parts[ch] if shift == 0 else pltpu.roll(parts[ch], shift, 1)
                chunk = jnp.where(group == ch, moved, chunk)
            send1[t * 4 + d4] = chunk.astype(BF16)

    def first(dst, src):
        return pltpu.make_async_remote_copy(
            src_ref=send1.at[dst], dst_ref=recv1.at[src], send_sem=s1.at[dst], recv_sem=r1.at[src],
            device_id=(dp, dst), device_id_type=MESH)

    def second(dst, src):
        return pltpu.make_async_remote_copy(
            src_ref=send2.at[dst], dst_ref=recv2.at[src], send_sem=s2.at[dst], recv_sem=r2.at[src],
            device_id=(dp, dst), device_id_type=MESH)

    self_head = jnp.logical_and(half == core, core == image)
    pl.semaphore_wait(barrier, SEQ - 1 + 2 + jnp.where(self_head, 2 * 15, 2 * 16))

    @pl.loop(1, SEQ)
    def _(k):
        first(lax.rem(me + k, SEQ), me).start()

    loads[5].start()
    recv1[me] = send1[me]

    @pl.loop(0, 8)
    def _(t):
        row = lax.broadcasted_iota(jnp.int32, (128, 128), 0) + t * 128
        odd, d, kt, a2 = row // 512, (row % 512) // 16, (row % 16) // 2, row % 2
        o = (2 * d + a2) * 14 + 2 * kt + odd
        near, far, share = taps(o, kt < 7, top, height)
        rows = pl.ds(pl.multiple_of(t * 128, 128), 128)
        for c in range(8):
            col = lax.broadcasted_iota(jnp.int32, (128, 128), 1) + c * 128
            w = jnp.where(col == near, 1.0 - share, 0.0) + jnp.where(col == far, share, 0.0)
            wrow[rows, c * 128 : c * 128 + 128] = w.astype(BF16)

    @pl.loop(1, SEQ)
    def _(k):
        first(me, lax.rem(me + k, SEQ)).wait_recv()

    x = recv1[...].reshape(1024, 128)
    low = lax.broadcasted_iota(jnp.int32, (256, 128), 1) < 64
    for i in range(2):
        h = lax.rem(me // 16 + 1 + i, 2)
        even = jnp.dot(wrow[pl.ds(pl.multiple_of(h * 256, 256), 256)], x, preferred_element_type=F32)
        odd = jnp.dot(wrow[pl.ds(pl.multiple_of(h * 256 + 512, 256), 256)], x, preferred_element_type=F32)
        to = pl.ds(h * 16, 16)
        send2[to, 0] = jnp.where(low, even, pltpu.roll(odd, 64, 1)).astype(BF16).reshape(16, 16, 128)
        send2[to, 1] = jnp.where(low, pltpu.roll(even, 64, 1), odd).astype(BF16).reshape(16, 16, 128)

        @pl.loop(i, 16)
        def _(k):
            second(h * 16 + lax.rem(me + k, 16), me).start()

    for one in other:
        one.start()
    recv2[me] = send2[me]

    for one in loads[3:5]:
        one.wait()

    @pl.loop(0, 7)
    def _(t):
        rho = lax.broadcasted_iota(jnp.int32, (128, 588), 0) + t * 128
        i, ch, j = rho // 64, (rho % 64) // 16, rho % 16
        origin = jnp.where(jnp.logical_and(ch < 3, j < 14), ch * 196 + i * 14 + j, -1)
        kappa = lax.broadcasted_iota(jnp.int32, (128, 588), 1)
        pick = jnp.where(origin == kappa, 1.0, 0.0).astype(BF16)
        rows = pl.ds(pl.multiple_of(t * 128, 128), 128)
        embw[rows, :] = jnp.dot(pick, emb[...], preferred_element_type=F32).astype(BF16)

    mine[0, HEAD:, :] = jnp.zeros((16, 2048), BF16)
    mine[1, HEAD:, :] = jnp.zeros((16, 2048), BF16)
    mine[2, HEAD:, :] = jnp.ones((16, 2048), BF16)

    @pl.loop(1, SEQ)
    def _(k):
        first(lax.rem(me + k, SEQ), me).wait_send()
        second(me, lax.rem(me + k, SEQ)).wait_recv()

    wide[...] = recv2[...].reshape(1024, 128).astype(F32)
    for kt in range(7):
        for a2 in range(2):
            piece = wide[pl.ds(kt * 2 + a2, 64, stride=16), :]
            tokens[a2 * 64 : a2 * 64 + 64, kt * 128 : kt * 128 + 128] = piece.astype(BF16)

    embedded[...] = jnp.dot(tokens[...], embw[...], preferred_element_type=F32) + pos[...].astype(F32)
    normed[...] = layer_norm(embedded[...], gain_attn[...].reshape(1, WIDTH))

    def head_rows(h):
        return pl.ds(pl.multiple_of(h * HEAD, 16), HEAD)

    def lanes(i):
        return pl.ds(pl.multiple_of(i * TOK, TOK), TOK)

    def span(t):
        return pl.ds(t, 1 + t)

    def inward(t, h, i):
        return pltpu.make_async_remote_copy(
            src_ref=flat.at[span(t), head_rows(h), :], dst_ref=mine.at[span(t), pl.ds(0, HEAD), lanes(i)],
            send_sem=s_in.at[t, h], recv_sem=r_in.at[t, i],
            device_id=(to_dp, to_seq + h), device_id_type=MESH)

    def backward(i, h):
        return pltpu.make_async_remote_copy(
            src_ref=back.at[i], dst_ref=heads.at[head_rows(h), :],
            send_sem=s_back.at[i], recv_sem=r_back.at[h],
            device_id=(from_dp, 2 * i + core), device_id_type=MESH)

    def turn(k):
        return lax.rem(slot // 4 + k // 4, 4) * 4 + lax.rem(slot + k, 4)

    def post(ts, first_k, last_k):
        @pl.loop(first_k, last_k)
        def _(k):
            h = turn(k)

            @pl.when(is_me(to_dp, to_seq + h))
            def _():
                for t in ts:
                    pltpu.make_async_copy(
                        flat.at[span(t), head_rows(h), :], mine.at[span(t), pl.ds(0, HEAD), lanes(slot)],
                        r_in.at[t, slot]).start()

            @pl.when(jnp.logical_not(is_me(to_dp, to_seq + h)))
            def _():
                for t in ts:
                    inward(t, h, slot).start()

    def posted(ts, first_k, last_k):
        @pl.loop(first_k, last_k)
        def _(k):
            h = turn(k)

            @pl.when(jnp.logical_not(is_me(to_dp, to_seq + h)))
            def _():
                for t in ts:
                    inward(t, h, slot).wait_send()

    def project(t, scale):
        proj = jnp.dot(normed[...], qkv[:, t * WIDTH : (t + 1) * WIDTH], preferred_element_type=F32)
        if scale is not None:
            proj = proj * scale
        for j in range(10):
            flat[t, j * 128 : j * 128 + 128, :] = proj[:, j * 128 : j * 128 + 128].T.astype(BF16)

    loads[5].wait()
    project(0, math.log2(math.e) / math.sqrt(HEAD))
    post((0,), 0, 16)
    project(1, None)
    project(2, None)
    post((1,), 0, 4)

    @pl.loop(1, SEQ)
    def _(k):
        second(lax.rem(me + k, SEQ), me).wait_send()

    posted((0,), 0, 16)
    post((1,), 4, 8)

    def keys_of(g):
        return pl.ds(pl.multiple_of(g * KB, KB), KB)

    def swap(g):
        return pltpu.make_async_remote_copy(
            src_ref=mine.at[pl.ds(1, 2), :, keys_of(g)], dst_ref=theirs.at[:, :, keys_of(g)],
            send_sem=s_swap.at[g], recv_sem=r_swap.at[g], device_id=sibling, device_id_type=MESH)

    @pl.loop(0, HEADS)
    def _(i):
        inward(0, 0, i).wait_recv()

    peak[...] = jnp.full((8, 2048), -jnp.inf, F32)
    acc[...] = jnp.zeros((96, 2048), F32)

    def group(step):
        return lax.rem(head // 4 + 4 - step, 4)

    def take(keys, values, q, old, sums):
        rows = keys.astype(F32).T.astype(BF16)
        s = jnp.dot(rows, q, preferred_element_type=F32)
        new = jnp.maximum(old, jnp.max(s, axis=0, keepdims=True))
        p = jnp.exp2(s - new).astype(BF16)
        return new, sums * jnp.exp2(old - new) + jnp.dot(values, p, preferred_element_type=F32)

    def arrived(g):
        for j in range(4):
            inward(1, 0, g * 4 + j).wait_recv()
        swap(g).start()

    def keep(new, sums):
        acc[...] = sums
        peak[...] = jnp.broadcast_to(new, (8, 2048))

    posted((1,), 0, 4)
    post((1,), 8, 12)
    begin = group(0)
    arrived(begin)
    keep(*take(mine[1, :, keys_of(begin)], mine[2, :, keys_of(begin)], mine[0], peak[:1, :], acc[...]))

    @pl.loop(1, 4)
    def _(step):
        @pl.when(step == 1)
        def _():
            posted((1,), 4, 8)
            post((1,), 12, 16)

        g, earlier = group(step), group(step - 1)
        arrived(g)
        swap(earlier).wait_recv()
        keep(*take(
            jnp.concatenate([theirs[0, :, keys_of(earlier)], mine[1, :, keys_of(g)]], axis=1),
            jnp.concatenate([theirs[1, :, keys_of(earlier)], mine[2, :, keys_of(g)]], axis=1),
            mine[0], peak[:1, :], acc[...]))

    for one in loads[6:]:
        one.start()
    last = group(3)
    swap(last).wait_recv()
    for step in range(2048 // QB):
        b = lax.rem(step + head, 2048 // QB)
        here = pl.ds(pl.multiple_of(b * QB, QB), QB)
        _, o = take(
            theirs[0, :, keys_of(last)], theirs[1, :, keys_of(last)], mine[0, :, here], peak[:1, here],
            acc[:, here])
        o = (o[:HEAD] / o[HEAD : HEAD + 1]).astype(BF16)
        for j in range(QB // TOK):
            back[b * (QB // TOK) + j] = o[:, j * TOK : j * TOK + TOK]

        @pl.loop(0, QB // TOK)
        def _(j):
            i = b * (QB // TOK) + lax.rem(j + head, QB // TOK)

            @pl.when(is_me(from_dp, 2 * i + core))
            def _():
                pltpu.make_async_copy(back.at[i], heads.at[head_rows(head), :], r_back.at[head]).start()

            @pl.when(jnp.logical_not(is_me(from_dp, 2 * i + core)))
            def _():
                backward(i, head).start()

    for one in loads[6:]:
        one.wait()

    @pl.loop(0, HEADS)
    def _(h):
        backward(0, h).wait_recv()

    attended = jnp.concatenate(
        [heads[j * 128 : j * 128 + 128, :].astype(F32).T.astype(BF16) for j in range(10)], axis=1)
    middle = embedded[...] + jnp.dot(attended, outw[...], preferred_element_type=F32)
    embedded[...] = middle
    normed[...] = layer_norm(middle, gain_mlp[...].reshape(1, WIDTH))

    def chunk(c):
        return pl.ds(c * ROWS, ROWS)

    def to_far(c):
        return remote(normed.at[chunk(c)], far_tok.at[chunk(c)], s_far.at[c], r_far.at[c], partner)

    parts = (pl.ds(0, 768), pl.ds(768, 512))

    def send_sum(c, k):
        return remote(
            giveback.at[chunk(c), parts[k]], fromfar.at[chunk(c), parts[k]], s_gb.at[c, k], r_gb.at[c, k], partner)

    def hidden_of(x):
        return [gelu(jnp.dot(x, up[...], preferred_element_type=F32)).astype(BF16) for up in (upw, upw2)]

    def summed(hidden, part):
        return jnp.dot(hidden[0], downw[:, part], preferred_element_type=F32) + jnp.dot(
            hidden[1], downw2[:, part], preferred_element_type=F32)

    for c in range(CHUNKS):
        to_far(c).start()
    for one in other:
        one.wait_recv()
    total[...] = embedded[...] + summed(hidden_of(normed[...]), slice(None))
    for c in range(CHUNKS):
        to_far(c).wait_recv()
        hidden = hidden_of(far_tok[chunk(c), :])
        for k, part in enumerate(parts):
            giveback[chunk(c), part] = summed(hidden, part).astype(BF16)
            send_sum(c, k).start()
    for c in range(CHUNKS):
        for k in range(2):
            send_sum(c, k).wait_recv()
        result[chunk(c), :] = (total[chunk(c), :] + fromfar[chunk(c), :].astype(F32)).astype(BF16)

    posted((1,), 8, 16)
    for one in other:
        one.wait_send()
    for g in range(4):
        swap(g).wait_send()
    for c in range(CHUNKS):
        to_far(c).wait_send()
        for k in range(2):
            send_sum(c, k).wait_send()

    @pl.loop(0, HEADS)
    def _(h):
        @pl.when(jnp.logical_not(is_me(from_dp, 2 * h + core)))
        def _():
            backward(h, 0).wait_send()


def shards(images, boxes, w_embed, pos_embed, gain_attn, w_qkv, w_attn_out, gain_mlp, w_up, w_down):
    vmem = pl.BlockSpec(memory_space=pltpu.VMEM)
    hbm = pl.BlockSpec(memory_space=pl.ANY)
    sem = pltpu.SemaphoreType.DMA
    V = pltpu.VMEM
    out = pl.pallas_call(
        layer_kernel,
        out_shape=jax.ShapeDtypeStruct((TOK, WIDTH), BF16),
        in_specs=[hbm] * 10,
        out_specs=vmem,
        scratch_shapes=[
            pltpu.SMEM((4, 4), jnp.int32), V((WIDTH,), F32), V((WIDTH,), F32), sem((3,)),
            V((96, 1024), BF16), V((588, WIDTH), BF16), V((TOK, WIDTH), BF16), V((WIDTH, 3 * WIDTH), BF16),
            V((WIDTH, WIDTH), BF16), V((WIDTH, WIDTH), BF16), V((WIDTH, WIDTH), BF16), sem((9,)),
            V((1024, 1024), BF16), V((96, 1024), F32), V((SEQ, 32, 128), BF16), V((SEQ, 32, 128), BF16),
            V((1024, 1024), BF16), V((SEQ, 2, 16, 128), BF16), V((SEQ, 2, 16, 128), BF16),
            V((1024, 128), F32), V((TOK, OUT), BF16), V((OUT, WIDTH), BF16), V((TOK, WIDTH), F32),
            sem((SEQ,)), sem((SEQ,)), sem((SEQ,)), sem((SEQ,)),
            V((3, WIDTH, TOK), BF16), V((3, 96, 2048), BF16), V((2, 96, 2048), BF16),
            V((96, 2048), F32), V((8, 2048), F32), V((16, HEAD, TOK), BF16), V((WIDTH, TOK), BF16),
            sem((2, 16)), sem((2, 16)), sem((4,)), sem((4,)), sem((16,)), sem((16,)),
            V((TOK, WIDTH), BF16), V((TOK, WIDTH), BF16), V((TOK, WIDTH), F32), V((TOK, WIDTH), BF16),
            V((TOK, WIDTH), BF16), V((WIDTH, WIDTH), BF16), V((WIDTH, WIDTH), BF16),
            sem((CHUNKS,)), sem((CHUNKS,)), sem((CHUNKS, 2)), sem((CHUNKS, 2)), sem((2,)), sem((2,)),
        ],
        compiler_params=pltpu.CompilerParams(
            collective_id=0, has_side_effects=True, vmem_limit_bytes=60 * 1024 * 1024),
        name="layer",
    )(boxes, images, w_embed, pos_embed, gain_attn, w_qkv, w_attn_out, gain_mlp, w_up, w_down)
    return out[None]


def solution(mesh):
    return jax.shard_map(
        shards,
        mesh=mesh,
        in_specs=(
            P("dp", None, "seq", None), P(), P(), P("seq", None), P(), P(), P(), P(),
            P(None, "dp"), P("dp", None),
        ),
        out_specs=P("dp", "seq", None),
        check_vma=False,
    )
```
